32 devices in a mesh: dp: 8 (over z, y), mp: 4 (over x, core).
Axes of the slice: x: 2, y: 2, z: 4, core: 2. Of those that a mesh axis runs over, the one named last changes fastest.
Arguments:
- image_emb: bfloat16 [6144, 1152], P(('dp', 'mp')), may hold values from -0.1875 to 0.1875
- text_emb: bfloat16 [6144, 1152], P(('dp', 'mp')), may hold values from -0.1875 to 0.1875
- log_scale: float32 [1], replicated, may hold values from 1.6 to 3
- bias: float32 [1], replicated, may hold values from -4 to -1
Outputs:
- image_grad: float32 [6144, 1152], P(('dp', 'mp'))
- text_grad: float32 [6144, 1152], P(('dp', 'mp'))
The draws below stay inside these ranges and needn't reach their ends.
All inputs are finite; a program needn't handle non-finite values.
Results may differ from the reference program's by a relative error of at most 0.0033.
Values may be sent and summed in bfloat16 or wider, within the bound.
A program may use at most 64 MiB of HBM per device.

```python
import jax
import jax.numpy as jnp

D = 1152
ROWS = 192
SHIFTS = 4
BLOCKS = 32
PAIRS = 6144


def level_of(own_key, dims, split, low, high):
    def one(position, shards_of):
        steps = jax.random.uniform(jax.random.fold_in(jax.random.fold_in(own_key, 6), position), (shards_of,), jnp.float32, low / len(split), high / len(split))
        return jnp.repeat(jnp.exp(steps), dims[position] // shards_of).reshape((-1,) + (1,) * (len(dims) - position - 1))

    loudness = one(*split[0])
    for cut in split[1:]:
        loudness = loudness * one(*cut)
    return loudness


def bell_draw(own_key, dims, spread, reach, shards=(), kind=jnp.bfloat16):
    drawn = jax.random.normal(own_key, dims, jnp.float32) * spread
    if len(shards) > 0:
        drawn = level_of(own_key, dims, shards, -0.22, 0.18) * drawn
    return jnp.clip(drawn, min=-reach, max=reach).astype(kind)


def setup_inputs(seed: int = 0) -> dict:
    keys = jax.random.split(jax.random.key(seed), 5)
    return {
        "image_emb": bell_draw(keys[0], (PAIRS, D), D ** -0.5, 0.1875, ((0, 32),)),
        "text_emb": bell_draw(keys[1], (PAIRS, D), D ** -0.5, 0.1875, ((0, 32),)),
        "log_scale": jnp.clip(jax.random.uniform(keys[2], (1,), jnp.float32, 1.6, 3.0), 1.6, 3.0),
        "bias": jnp.clip(jax.random.uniform(keys[3], (1,), jnp.float32, -4.0, -1.0), -4.0, -1.0),
    }


def reference(image_emb, text_emb, log_scale, bias):
    scale = jnp.exp(log_scale[0])
    offset = bias[0]
    images = image_emb.astype(jnp.float32).reshape(BLOCKS, ROWS, D)
    texts = text_emb.astype(jnp.float32).reshape(BLOCKS, ROWS, D)
    image_grad = jnp.zeros((BLOCKS, ROWS, D), jnp.float32)
    text_grad = jnp.zeros((BLOCKS, ROWS, D), jnp.float32)
    identity = jnp.eye(ROWS, dtype=jnp.float32)
    for step in range(SHIFTS + 1):
        moved = jnp.roll(texts, step, axis=0)
        logits = scale * jnp.einsum("nrd,ncd->nrc", images, moved) + offset
        target = identity if step == 0 else jnp.zeros_like(identity)
        weights = (scale * (jax.nn.sigmoid(logits) - target)).astype(jnp.bfloat16).astype(jnp.float32)
        image_grad = image_grad + jnp.einsum("nrc,ncd->nrd", weights, moved)
        text_grad = text_grad + jnp.roll(jnp.einsum("nrc,nrd->ncd", weights, images), -step, axis=0)
    return image_grad.reshape(PAIRS, D), text_grad.reshape(PAIRS, D)
```

```python
import jax
import jax.numpy as jnp
from jax import lax
from jax.experimental import pallas as pl
from jax.experimental.pallas import tpu as pltpu
from jax.sharding import PartitionSpec as P

SHIFTS = 4
CHUNKS = 4

FAR = 0
NEAR_OWN, NEAR_FAR = 2, 3
CORE_OWN, CORE_FAR, CORE_NEAR_OWN, CORE_NEAR_FAR = 4, 5, 6, 7


def kernel(log_scale_ref, bias_ref, image_ref, text_ref, image_out, text_out, own, held, total, load_sem, send_sem, recv_sem):
    dp_count, mp_count = lax.axis_size("dp"), lax.axis_size("mp")
    count = dp_count * mp_count
    me = lax.axis_index("dp") * mp_count + lax.axis_index("mp")
    core = lax.rem(me, 2)
    side = lax.rem(me // 2, 2)
    rows = image_ref.shape[0]
    part = rows // CHUNKS

    def place(index):
        return (index // mp_count, lax.rem(index, mp_count))

    after = place(lax.rem(me + SHIFTS, count))
    before = place(lax.rem(me + count - SHIFTS, count))
    near = place(me + 2 - 4 * side)
    twin = place(me + 1 - 2 * core)

    loads = [
        pltpu.make_async_copy(image_ref, own.at[0], load_sem.at[0]),
        pltpu.make_async_copy(text_ref, own.at[1], load_sem.at[1]),
    ]
    for load in loads:
        load.start()

    barrier = pltpu.get_barrier_semaphore()
    for other in (after, before, near, twin):
        pl.semaphore_signal(barrier, inc=1, device_id=other, device_id_type=pl.DeviceIdType.MESH)
    pl.semaphore_wait(barrier, 4)
    for load in loads:
        load.wait()

    def remote(source, slot, chunk, device):
        span = pl.ds(chunk * part, part)
        return pltpu.make_async_remote_copy(
            src_ref=source.at[span],
            dst_ref=held.at[slot, span],
            send_sem=send_sem.at[slot, chunk],
            recv_sem=recv_sem.at[slot, chunk],
            device_id=device,
            device_id_type=pl.DeviceIdType.MESH,
        )

    def far(kind, chunk):
        target = tuple(jnp.where(kind == 0, b, a) for a, b in zip(after, before))
        return remote(own.at[kind], FAR + kind, chunk, target)

    first, second = side, 1 - side
    near_own = [remote(own.at[1 - side], NEAR_OWN, i, near) for i in range(CHUNKS)]
    near_far = [remote(held.at[FAR + side], NEAR_FAR, i, near) for i in range(CHUNKS)]
    core_own = [remote(own.at[1 - core], CORE_OWN, i, twin) for i in range(CHUNKS)]
    core_far = [remote(held.at[FAR + core], CORE_FAR, i, twin) for i in range(CHUNKS)]
    core_near_own = [remote(held.at[NEAR_OWN], CORE_NEAR_OWN, i, twin) for i in range(CHUNKS)]
    core_near_far = [remote(held.at[NEAR_FAR], CORE_NEAR_FAR, i, twin) for i in range(CHUNKS)]
    far_first = [far(first, i) for i in range(CHUNKS)]
    far_second = [far(second, i) for i in range(CHUNKS)]

    for i in range(CHUNKS):
        far_first[i].start()
        near_own[i].start()
    for i in range(CHUNKS):
        far_second[i].start()
        core_own[i].start()

    scale = jnp.exp(jnp.full((1, rows), log_scale_ref[0], jnp.float32))
    offset = bias_ref[0]

    def weights_of(mine, block):
        inner = lax.dot_general(mine, block, (((1,), (1,)), ((), ())), preferred_element_type=jnp.float32)
        return jax.nn.sigmoid(scale * inner + offset)

    def add(slot, kind):
        block = held[slot]
        weights = (scale * weights_of(own[1 - kind], block)).astype(jnp.bfloat16)
        total[1 - kind] += jnp.dot(weights, block, preferred_element_type=jnp.float32)

    row_ids = lax.broadcasted_iota(jnp.int32, (rows, rows), 0)
    col_ids = lax.broadcasted_iota(jnp.int32, (rows, rows), 1)
    target = jnp.where(row_ids == col_ids, 1.0, 0.0).astype(jnp.float32)
    own_weights = (scale * (weights_of(own[0], own[1]) - target)).astype(jnp.bfloat16)
    total[0] = jnp.dot(own_weights, own[1], preferred_element_type=jnp.float32)
    total[1] = lax.dot_general(own_weights, own[0], (((0,), (0,)), ((), ())), preferred_element_type=jnp.float32)

    for copy in core_own:
        copy.wait_recv()
    add(CORE_OWN, core)

    for i in range(CHUNKS):
        far_first[i].wait_recv()
        near_far[i].start()

        @pl.when(side == core)
        def _():
            core_far[i].start()

    add(FAR + first, first)

    for i in range(CHUNKS):
        near_own[i].wait_recv()
        core_near_own[i].start()
    add(NEAR_OWN, side)
    for copy in core_near_own:
        copy.wait_recv()
    add(CORE_NEAR_OWN, side)

    for i in range(CHUNKS):
        far_second[i].wait_recv()

        @pl.when(side != core)
        def _():
            core_far[i].start()

        near_far[i].wait_recv()
        core_near_far[i].start()

    add(FAR + second, second)
    add(NEAR_FAR, 1 - side)
    for copy in core_far:
        copy.wait_recv()
    add(CORE_FAR, 1 - core)
    for copy in core_near_far:
        copy.wait_recv()
    add(CORE_NEAR_FAR, 1 - side)

    stores = [
        pltpu.make_async_copy(total.at[0], image_out, load_sem.at[0]),
        pltpu.make_async_copy(total.at[1], text_out, load_sem.at[1]),
    ]
    for store in stores:
        store.start()
    for copies in (far_first, far_second, near_own, near_far, core_own, core_far, core_near_own, core_near_far):
        for copy in copies:
            copy.wait_send()
    for store in stores:
        store.wait()


def local(image_emb, text_emb, log_scale, bias):
    rows, width = image_emb.shape
    block = jax.ShapeDtypeStruct((rows, width), jnp.float32)
    return pl.pallas_call(
        kernel,
        out_shape=(block, block),
        in_specs=[
            pl.BlockSpec(memory_space=pltpu.SMEM),
            pl.BlockSpec(memory_space=pltpu.SMEM),
            pl.BlockSpec(memory_space=pl.ANY),
            pl.BlockSpec(memory_space=pl.ANY),
        ],
        out_specs=(pl.BlockSpec(memory_space=pl.ANY), pl.BlockSpec(memory_space=pl.ANY)),
        scratch_shapes=[
            pltpu.VMEM((2, rows, width), jnp.bfloat16),
            pltpu.VMEM((8, rows, width), jnp.bfloat16),
            pltpu.VMEM((2, rows, width), jnp.float32),
            pltpu.SemaphoreType.DMA((2,)),
            pltpu.SemaphoreType.DMA((8, CHUNKS)),
            pltpu.SemaphoreType.DMA((8, CHUNKS)),
        ],
        compiler_params=pltpu.CompilerParams(
            collective_id=0, has_side_effects=True, vmem_limit_bytes=32 * 1024 * 1024
        ),
        cost_estimate=pl.CostEstimate(
            flops=20 * 2 * rows * rows * width, bytes_accessed=12 * rows * width, transcendentals=9 * rows * rows
        ),
    )(log_scale, bias, image_emb, text_emb)


def solution(mesh):
    count = 1
    for axis in ("dp", "mp"):
        count *= mesh.shape[axis]
    assert mesh.shape["mp"] % 4 == 0 and count > 2 * SHIFTS
    return jax.shard_map(
        local,
        mesh=mesh,
        in_specs=(P(("dp", "mp"), None), P(("dp", "mp"), None), P(), P()),
        out_specs=(P(("dp", "mp"), None), P(("dp", "mp"), None)),
        check_vma=False,
    )
```

```python
import jax
import jax.numpy as jnp
from jax import lax
from jax.experimental import pallas as pl
from jax.experimental.pallas import tpu as pltpu
from jax.sharding import PartitionSpec as P

SHIFTS = 4
CHUNKS = 4

FAR = 0
NEAR_OWN, NEAR_FAR = 2, 3
CORE_OWN, CORE_FAR, CORE_NEAR_OWN, CORE_NEAR_FAR = 4, 5, 6, 7


def kernel(log_scale_ref, bias_ref, image_ref, text_ref, image_out, text_out, own, held, total, load_sem, send_sem, recv_sem):
    dp_count, mp_count = lax.axis_size("dp"), lax.axis_size("mp")
    count = dp_count * mp_count
    me = lax.axis_index("dp") * mp_count + lax.axis_index("mp")
    core = lax.rem(me, 2)
    side = lax.rem(me // 2, 2)
    rows = image_ref.shape[0]
    part = rows // CHUNKS

    def place(index):
        return (index // mp_count, lax.rem(index, mp_count))

    after = place(lax.rem(me + SHIFTS, count))
    before = place(lax.rem(me + count - SHIFTS, count))
    near = place(me + 2 - 4 * side)
    twin = place(me + 1 - 2 * core)

    loads = [
        pltpu.make_async_copy(image_ref, own.at[0], load_sem.at[0]),
        pltpu.make_async_copy(text_ref, own.at[1], load_sem.at[1]),
    ]
    for load in loads:
        load.start()

    barrier = pltpu.get_barrier_semaphore()
    for other in (after, before, near, twin):
        pl.semaphore_signal(barrier, inc=1, device_id=other, device_id_type=pl.DeviceIdType.MESH)
    pl.semaphore_wait(barrier, 4)
    for load in loads:
        load.wait()

    def remote(source, slot, chunk, device):
        span = pl.ds(chunk * part, part)
        return pltpu.make_async_remote_copy(
            src_ref=source.at[span],
            dst_ref=held.at[slot, span],
            send_sem=send_sem.at[slot, chunk],
            recv_sem=recv_sem.at[slot, chunk],
            device_id=device,
            device_id_type=pl.DeviceIdType.MESH,
        )

    def far(kind, chunk):
        target = tuple(jnp.where(kind == 0, b, a) for a, b in zip(after, before))
        return remote(own.at[kind], FAR + kind, chunk, target)

    first, second = side, 1 - side
    near_own = [remote(own.at[1 - side], NEAR_OWN, i, near) for i in range(CHUNKS)]
    near_far = [remote(held.at[FAR + side], NEAR_FAR, i, near) for i in range(CHUNKS)]
    core_own = [remote(own.at[1 - core], CORE_OWN, i, twin) for i in range(CHUNKS)]
    core_far = [remote(held.at[FAR + core], CORE_FAR, i, twin) for i in range(CHUNKS)]
    core_near_own = [remote(held.at[NEAR_OWN], CORE_NEAR_OWN, i, twin) for i in range(CHUNKS)]
    core_near_far = [remote(held.at[NEAR_FAR], CORE_NEAR_FAR, i, twin) for i in range(CHUNKS)]
    far_first = [far(first, i) for i in range(CHUNKS)]
    far_second = [far(second, i) for i in range(CHUNKS)]

    for i in range(CHUNKS):
        far_first[i].start()
        near_own[i].start()
    for i in range(CHUNKS):
        core_own[i].start()

    scale = jnp.exp(jnp.full((1, rows), log_scale_ref[0], jnp.float32))
    offset = bias_ref[0]

    def weights_of(mine, block):
        inner = lax.dot_general(mine, block, (((1,), (1,)), ((), ())), preferred_element_type=jnp.float32)
        return jax.nn.sigmoid(scale * inner + offset)

    def add(slot, kind):
        block = held[slot]
        weights = (scale * weights_of(own[1 - kind], block)).astype(jnp.bfloat16)
        total[1 - kind] += jnp.dot(weights, block, preferred_element_type=jnp.float32)

    row_ids = lax.broadcasted_iota(jnp.int32, (rows, rows), 0)
    col_ids = lax.broadcasted_iota(jnp.int32, (rows, rows), 1)
    target = jnp.where(row_ids == col_ids, 1.0, 0.0).astype(jnp.float32)
    own_weights = (scale * (weights_of(own[0], own[1]) - target)).astype(jnp.bfloat16)
    total[0] = jnp.dot(own_weights, own[1], preferred_element_type=jnp.float32)
    total[1] = lax.dot_general(own_weights, own[0], (((0,), (0,)), ((), ())), preferred_element_type=jnp.float32)

    for copy in core_own:
        copy.wait_recv()
    add(CORE_OWN, core)

    for i in range(CHUNKS):
        far_first[i].wait_recv()
        near_far[i].start()
        far_second[i].start()

        @pl.when(side == core)
        def _():
            core_far[i].start()

    add(FAR + first, first)

    for i in range(CHUNKS):
        near_own[i].wait_recv()
        core_near_own[i].start()
    add(NEAR_OWN, side)
    for copy in core_near_own:
        copy.wait_recv()
    add(CORE_NEAR_OWN, side)

    for i in range(CHUNKS):
        far_second[i].wait_recv()

        @pl.when(side != core)
        def _():
            core_far[i].start()

        near_far[i].wait_recv()
        core_near_far[i].start()

    add(FAR + second, second)
    add(NEAR_FAR, 1 - side)
    for copy in core_far:
        copy.wait_recv()
    add(CORE_FAR, 1 - core)
    for copy in core_near_far:
        copy.wait_recv()
    add(CORE_NEAR_FAR, 1 - side)

    stores = [
        pltpu.make_async_copy(total.at[0], image_out, load_sem.at[0]),
        pltpu.make_async_copy(total.at[1], text_out, load_sem.at[1]),
    ]
    for store in stores:
        store.start()
    for copies in (far_first, far_second, near_own, near_far, core_own, core_far, core_near_own, core_near_far):
        for copy in copies:
            copy.wait_send()
    for store in stores:
        store.wait()


def local(image_emb, text_emb, log_scale, bias):
    rows, width = image_emb.shape
    block = jax.ShapeDtypeStruct((rows, width), jnp.float32)
    return pl.pallas_call(
        kernel,
        out_shape=(block, block),
        in_specs=[
            pl.BlockSpec(memory_space=pltpu.SMEM),
            pl.BlockSpec(memory_space=pltpu.SMEM),
            pl.BlockSpec(memory_space=pl.ANY),
            pl.BlockSpec(memory_space=pl.ANY),
        ],
        out_specs=(pl.BlockSpec(memory_space=pl.ANY), pl.BlockSpec(memory_space=pl.ANY)),
        scratch_shapes=[
            pltpu.VMEM((2, rows, width), jnp.bfloat16),
            pltpu.VMEM((8, rows, width), jnp.bfloat16),
            pltpu.VMEM((2, rows, width), jnp.float32),
            pltpu.SemaphoreType.DMA((2,)),
            pltpu.SemaphoreType.DMA((8, CHUNKS)),
            pltpu.SemaphoreType.DMA((8, CHUNKS)),
        ],
        compiler_params=pltpu.CompilerParams(
            collective_id=0, has_side_effects=True, vmem_limit_bytes=60 * 1024 * 1024
        ),
        cost_estimate=pl.CostEstimate(
            flops=20 * 2 * rows * rows * width, bytes_accessed=12 * rows * width, transcendentals=9 * rows * rows
        ),
    )(log_scale, bias, image_emb, text_emb)


def solution(mesh):
    count = 1
    for axis in ("dp", "mp"):
        count *= mesh.shape[axis]
    assert mesh.shape["mp"] % 4 == 0 and count > 2 * SHIFTS
    return jax.shard_map(
        local,
        mesh=mesh,
        in_specs=(P(("dp", "mp"), None), P(("dp", "mp"), None), P(), P()),
        out_specs=(P(("dp", "mp"), None), P(("dp", "mp"), None)),
        check_vma=False,
    )
```

```python
import jax
import jax.numpy as jnp
from jax import lax
from jax.experimental import pallas as pl
from jax.experimental.pallas import tpu as pltpu
from jax.sharding import PartitionSpec as P

SHIFTS = 4
CHUNKS = 3

FAR_FIRST = 0
NEAR_OWN = 1
CORE_NEAR_OWN = 2
FAR_SECOND = 3
NEAR_FAR = 4
CORE_NEAR_FAR = 5
CORE_OWN = 6
CORE_FAR = 7


def kernel(
    log_scale_ref, bias_ref, image_ref, text_ref, total,
    own, turned, held, twin_held, load_sem, send_sem, recv_sem,
):
    dp_count, mp_count = lax.axis_size("dp"), lax.axis_size("mp")
    count = dp_count * mp_count
    me = lax.axis_index("dp") * mp_count + lax.axis_index("mp")
    core = lax.rem(me, 2)
    side = lax.rem(me // 2, 2)
    rows, width = image_ref.shape
    part = rows // CHUNKS

    def place(index):
        return (index // mp_count, lax.rem(index, mp_count))

    after = place(lax.rem(me + SHIFTS, count))
    before = place(lax.rem(me + count - SHIFTS, count))
    near = place(me + 2 - 4 * side)
    twin = place(me + 1 - 2 * core)

    loads = [
        pltpu.make_async_copy(image_ref, own.at[0], load_sem.at[0]),
        pltpu.make_async_copy(text_ref, own.at[1], load_sem.at[1]),
    ]
    for load in loads:
        load.start()

    barrier = pltpu.get_barrier_semaphore()
    for other in (after, before, near, twin):
        pl.semaphore_signal(barrier, inc=1, device_id=other, device_id_type=pl.DeviceIdType.MESH)
    pl.semaphore_wait(barrier, 4)
    for load in loads:
        load.wait()

    def remote(source, target, slot, chunk, device):
        return pltpu.make_async_remote_copy(
            src_ref=source,
            dst_ref=target,
            send_sem=send_sem.at[slot, chunk],
            recv_sem=recv_sem.at[slot, chunk],
            device_id=device,
            device_id_type=pl.DeviceIdType.MESH,
        )

    def span(chunk):
        return pl.ds(chunk * part, part)

    def far(kind, slot, chunk):
        device = tuple(jnp.where(kind == 0, b, a) for a, b in zip(after, before))
        return remote(own.at[kind, span(chunk)], held.at[chunk, slot], slot, chunk, device)

    first, second = side, 1 - side
    chunks = range(CHUNKS)
    far_first = [far(first, FAR_FIRST, i) for i in chunks]
    far_second = [far(second, FAR_SECOND, i) for i in chunks]
    near_own = [remote(own.at[1 - side, span(i)], held.at[i, NEAR_OWN], NEAR_OWN, i, near) for i in chunks]
    near_far = [remote(held.at[i, FAR_FIRST], held.at[i, NEAR_FAR], NEAR_FAR, i, near) for i in chunks]
    core_near_own = [remote(held.at[i, NEAR_OWN], held.at[i, CORE_NEAR_OWN], CORE_NEAR_OWN, i, twin) for i in chunks]
    core_near_far = [remote(held.at[i, NEAR_FAR], held.at[i, CORE_NEAR_FAR], CORE_NEAR_FAR, i, twin) for i in chunks]
    core_own = [remote(own.at[1 - core, span(i)], twin_held.at[0, span(i)], CORE_OWN, i, twin) for i in chunks]
    far_slot = jnp.where(side == core, FAR_FIRST, FAR_SECOND)
    core_far = [remote(held.at[i, far_slot], twin_held.at[1, span(i)], CORE_FAR, i, twin) for i in chunks]

    for i in chunks:
        far_first[i].start()
        near_own[i].start()
    for i in chunks:
        core_own[i].start()
    far_second[0].start()

    scale = jnp.exp(jnp.full((1, rows), log_scale_ref[0], jnp.float32))
    offset = bias_ref[0]
    for kind in range(2):
        turned[kind] = own[kind].T

    def weights_of(block, kind):
        inner = jnp.dot(block, turned[1 - kind], preferred_element_type=jnp.float32)
        return jax.nn.sigmoid(scale * inner + offset)

    def add(block, kind):
        weights = (scale * weights_of(block, kind)).astype(jnp.bfloat16)
        total[1 - kind] += lax.dot_general(
            weights, block, (((0,), (0,)), ((), ())), preferred_element_type=jnp.float32
        )

    row_ids = lax.broadcasted_iota(jnp.int32, (rows, rows), 0)
    col_ids = lax.broadcasted_iota(jnp.int32, (rows, rows), 1)
    target = jnp.where(row_ids == col_ids, 1.0, 0.0).astype(jnp.float32)
    own_weights = (scale * (weights_of(own[0], 0) - target)).astype(jnp.bfloat16)
    total[0] = jnp.dot(own_weights, own[1], preferred_element_type=jnp.float32)
    total[1] = lax.dot_general(own_weights, own[0], (((0,), (0,)), ((), ())), preferred_element_type=jnp.float32)

    for copy in core_own:
        copy.wait_recv()
    add(twin_held[0], core)

    for i in chunks:
        far_first[i].wait_recv()
        near_far[i].start()

        @pl.when(side == core)
        def _():
            core_far[i].start()

        if i + 1 < CHUNKS:
            far_second[i + 1].start()
        near_own[i].wait_recv()
        core_near_own[i].start()

    for i in chunks:
        core_near_own[i].wait_recv()
        add(held[i, 0:3].reshape(3 * part, width), side)

    for i in chunks:
        near_far[i].wait_recv()
        core_near_far[i].start()
        far_second[i].wait_recv()

        @pl.when(side != core)
        def _():
            core_far[i].start()

        if i + 1 == CHUNKS:
            for copy in core_far[:-1]:
                copy.wait_recv()
            add(twin_held[1, : rows - part], 1 - core)
        core_near_far[i].wait_recv()
        add(held[i, 3:6].reshape(3 * part, width), 1 - side)

    core_far[-1].wait_recv()
    add(twin_held[1, rows - part :], 1 - core)

    for copies in (far_first, far_second, near_own, near_far, core_own, core_far, core_near_own, core_near_far):
        for copy in copies:
            copy.wait_send()


def write_out(total, image_out, text_out, store_sem):
    stores = [
        pltpu.make_async_copy(total.at[0], image_out, store_sem.at[0]),
        pltpu.make_async_copy(total.at[1], text_out, store_sem.at[1]),
    ]
    for store in stores:
        store.start()
    for store in stores:
        store.wait()


def local(image_emb, text_emb, log_scale, bias):
    rows, width = image_emb.shape
    block = jax.ShapeDtypeStruct((rows, width), jnp.float32)
    part = rows // CHUNKS
    in_hbm = [pltpu.with_memory_space_constraint(value, pltpu.HBM) for value in (image_emb, text_emb)]
    total = pl.pallas_call(
        kernel,
        out_shape=pltpu.VMEM((2, rows, width), jnp.float32),
        in_specs=[pl.BlockSpec(memory_space=pltpu.SMEM)] * 2 + [pl.BlockSpec(memory_space=pl.ANY)] * 2,
        out_specs=pl.BlockSpec(memory_space=pltpu.VMEM),
        scratch_shapes=[
            pltpu.VMEM((2, rows, width), jnp.bfloat16),
            pltpu.VMEM((2, width, rows), jnp.bfloat16),
            pltpu.VMEM((CHUNKS, 6, part, width), jnp.bfloat16),
            pltpu.VMEM((2, rows, width), jnp.bfloat16),
            pltpu.SemaphoreType.DMA((2,)),
            pltpu.SemaphoreType.DMA((8, CHUNKS)),
            pltpu.SemaphoreType.DMA((8, CHUNKS)),
        ],
        compiler_params=pltpu.CompilerParams(
            collective_id=0, has_side_effects=True, vmem_limit_bytes=32 * 1024 * 1024
        ),
        cost_estimate=pl.CostEstimate(
            flops=20 * 2 * rows * rows * width, bytes_accessed=12 * rows * width, transcendentals=9 * rows * rows
        ),
    )(log_scale, bias, *in_hbm)
    return pl.pallas_call(
        write_out,
        out_shape=(block, block),
        in_specs=[pl.BlockSpec(memory_space=pltpu.VMEM)],
        out_specs=(pl.BlockSpec(memory_space=pl.ANY), pl.BlockSpec(memory_space=pl.ANY)),
        scratch_shapes=[pltpu.SemaphoreType.DMA((2,))],
        cost_estimate=pl.CostEstimate(flops=0, bytes_accessed=16 * rows * width, transcendentals=0),
    )(total)


def solution(mesh):
    count = 1
    for axis in ("dp", "mp"):
        count *= mesh.shape[axis]
    assert mesh.shape["mp"] % 4 == 0 and count > 2 * SHIFTS
    return jax.shard_map(
        local,
        mesh=mesh,
        in_specs=(P(("dp", "mp"), None), P(("dp", "mp"), None), P(), P()),
        out_specs=(P(("dp", "mp"), None), P(("dp", "mp"), None)),
        check_vma=False,
    )
```

```python
import jax
import jax.numpy as jnp
from jax import lax
from jax.experimental import pallas as pl
from jax.experimental.pallas import tpu as pltpu
from jax.sharding import PartitionSpec as P

SHIFTS = 4
SIZES = (32, 64, 64, 32)
STARTS = (0, 32, 96, 160)
CHUNKS = len(SIZES)
DEPTH = 2

FAR_FIRST = 0
NEAR_OWN = 1
CORE_NEAR_OWN = 2
FAR_SECOND = 3
NEAR_FAR = 4
CORE_NEAR_FAR = 5
CORE_OWN = 6
CORE_FAR = 7


def kernel(
    log_scale_ref, bias_ref, image_ref, text_ref, total,
    own, turned, *scratch,
):
    dp_count, mp_count = lax.axis_size("dp"), lax.axis_size("mp")
    count = dp_count * mp_count
    me = lax.axis_index("dp") * mp_count + lax.axis_index("mp")
    core = lax.rem(me, 2)
    side = lax.rem(me // 2, 2)
    rows, width = image_ref.shape
    held = scratch[:CHUNKS]
    twin_held, load_sem, send_sem, recv_sem = scratch[CHUNKS:]

    def place(index):
        return (index // mp_count, lax.rem(index, mp_count))

    after = place(lax.rem(me + SHIFTS, count))
    before = place(lax.rem(me + count - SHIFTS, count))
    near = place(me + 2 - 4 * side)
    twin = place(me + 1 - 2 * core)

    loads = [
        pltpu.make_async_copy(image_ref, own.at[0], load_sem.at[0]),
        pltpu.make_async_copy(text_ref, own.at[1], load_sem.at[1]),
    ]
    for load in loads:
        load.start()

    barrier = pltpu.get_barrier_semaphore()
    for other in (after, before, near, twin):
        pl.semaphore_signal(barrier, inc=1, device_id=other, device_id_type=pl.DeviceIdType.MESH)
    pl.semaphore_wait(barrier, 4)
    for load in loads:
        load.wait()

    def remote(source, target, slot, chunk, device):
        return pltpu.make_async_remote_copy(
            src_ref=source,
            dst_ref=target,
            send_sem=send_sem.at[slot, chunk],
            recv_sem=recv_sem.at[slot, chunk],
            device_id=device,
            device_id_type=pl.DeviceIdType.MESH,
        )

    def span(chunk):
        return pl.ds(STARTS[chunk], SIZES[chunk])

    def far(kind, slot, chunk):
        device = tuple(jnp.where(kind == 0, b, a) for a, b in zip(after, before))
        return remote(own.at[kind, span(chunk)], held[chunk].at[slot], slot, chunk, device)

    first, second = side, 1 - side
    chunks = range(CHUNKS)

    def passed(source, slot, device):
        return [remote(held[i].at[source], held[i].at[slot], slot, i, device) for i in chunks]

    far_stream = [far(first, FAR_FIRST, i) for i in chunks] + [far(second, FAR_SECOND, i) for i in chunks]
    near_stream = [remote(own.at[1 - side, span(i)], held[i].at[NEAR_OWN], NEAR_OWN, i, near) for i in chunks]
    near_stream += passed(FAR_FIRST, NEAR_FAR, near)
    twin_stream = passed(NEAR_OWN, CORE_NEAR_OWN, twin) + passed(NEAR_FAR, CORE_NEAR_FAR, twin)
    core_own = [remote(own.at[1 - core, span(i)], twin_held.at[0, span(i)], CORE_OWN, i, twin) for i in chunks]
    far_slot = jnp.where(side == core, FAR_FIRST, FAR_SECOND)
    core_far = [remote(held[i].at[far_slot], twin_held.at[1, span(i)], CORE_FAR, i, twin) for i in chunks]

    for i in range(DEPTH):
        far_stream[i].start()
        near_stream[i].start()
    for copy in core_own:
        copy.start()

    scale = jnp.exp(jnp.full((1, rows), log_scale_ref[0], jnp.float32))
    offset = bias_ref[0]
    for kind in range(2):
        turned[kind] = own[kind].T

    def weights_of(block, kind):
        inner = jnp.dot(block, turned[1 - kind], preferred_element_type=jnp.float32)
        return jax.nn.sigmoid(scale * inner + offset)

    def add(block, kind):
        weights = (scale * weights_of(block, kind)).astype(jnp.bfloat16)
        total[1 - kind] += lax.dot_general(
            weights, block, (((0,), (0,)), ((), ())), preferred_element_type=jnp.float32
        )

    def add_batch(step):
        twin_stream[step].wait_recv()
        chunk, late = step % CHUNKS, step // CHUNKS
        block = held[chunk][3 * late : 3 * late + 3].reshape(3 * SIZES[chunk], width)
        add(block, second if late else first)

    row_ids = lax.broadcasted_iota(jnp.int32, (rows, rows), 0)
    col_ids = lax.broadcasted_iota(jnp.int32, (rows, rows), 1)
    target = jnp.where(row_ids == col_ids, 1.0, 0.0).astype(jnp.float32)
    own_weights = (scale * (weights_of(own[0], 0) - target)).astype(jnp.bfloat16)
    total[0] = jnp.dot(own_weights, own[1], preferred_element_type=jnp.float32)
    total[1] = lax.dot_general(own_weights, own[0], (((0,), (0,)), ((), ())), preferred_element_type=jnp.float32)

    steps = 2 * CHUNKS
    for step in range(steps):
        far_stream[step].wait_send()
        if step + DEPTH < steps:
            far_stream[step + DEPTH].start()
        near_stream[step].wait_send()
        if step + DEPTH < steps:
            near_stream[step + DEPTH].start()
        near_stream[step].wait_recv()
        twin_stream[step].start()
        far_stream[step].wait_recv()

        @pl.when((side == core) if step < CHUNKS else (side != core))
        def _():
            core_far[step % CHUNKS].start()

        if step == 0:
            for copy in core_own:
                copy.wait_recv()
            add(twin_held[0], core)
        else:
            add_batch(step - 1)

    early = STARTS[-1]
    for copy in core_far[:-1]:
        copy.wait_recv()
    add(twin_held[1, :early], 1 - core)
    add_batch(steps - 1)
    core_far[-1].wait_recv()
    add(twin_held[1, early:], 1 - core)

    for copies in (twin_stream, core_own, core_far):
        for copy in copies:
            copy.wait_send()


def write_out(total, image_out, text_out, store_sem):
    stores = [
        pltpu.make_async_copy(total.at[0], image_out, store_sem.at[0]),
        pltpu.make_async_copy(total.at[1], text_out, store_sem.at[1]),
    ]
    for store in stores:
        store.start()
    for store in stores:
        store.wait()


def local(image_emb, text_emb, log_scale, bias):
    rows, width = image_emb.shape
    block = jax.ShapeDtypeStruct((rows, width), jnp.float32)
    assert rows == sum(SIZES)
    in_hbm = [pltpu.with_memory_space_constraint(value, pltpu.HBM) for value in (image_emb, text_emb)]
    total = pl.pallas_call(
        kernel,
        out_shape=pltpu.VMEM((2, rows, width), jnp.float32),
        in_specs=[pl.BlockSpec(memory_space=pltpu.SMEM)] * 2 + [pl.BlockSpec(memory_space=pl.ANY)] * 2,
        out_specs=pl.BlockSpec(memory_space=pltpu.VMEM),
        scratch_shapes=[
            pltpu.VMEM((2, rows, width), jnp.bfloat16),
            pltpu.VMEM((2, width, rows), jnp.bfloat16),
            *[pltpu.VMEM((6, size, width), jnp.bfloat16) for size in SIZES],
            pltpu.VMEM((2, rows, width), jnp.bfloat16),
            pltpu.SemaphoreType.DMA((2,)),
            pltpu.SemaphoreType.DMA((8, CHUNKS)),
            pltpu.SemaphoreType.DMA((8, CHUNKS)),
        ],
        compiler_params=pltpu.CompilerParams(
            collective_id=0, has_side_effects=True, vmem_limit_bytes=32 * 1024 * 1024
        ),
        cost_estimate=pl.CostEstimate(
            flops=20 * 2 * rows * rows * width, bytes_accessed=12 * rows * width, transcendentals=9 * rows * rows
        ),
    )(log_scale, bias, *in_hbm)
    return pl.pallas_call(
        write_out,
        out_shape=(block, block),
        in_specs=[pl.BlockSpec(memory_space=pl.ANY)],
        out_specs=(pl.BlockSpec(memory_space=pl.ANY), pl.BlockSpec(memory_space=pl.ANY)),
        scratch_shapes=[pltpu.SemaphoreType.DMA((2,))],
        compiler_params=pltpu.CompilerParams(vmem_limit_bytes=1024 * 1024),
        cost_estimate=pl.CostEstimate(flops=0, bytes_accessed=16 * rows * width, transcendentals=0),
    )(total)


def solution(mesh):
    count = 1
    for axis in ("dp", "mp"):
        count *= mesh.shape[axis]
    assert mesh.shape["mp"] % 4 == 0 and count > 2 * SHIFTS
    return jax.shard_map(
        local,
        mesh=mesh,
        in_specs=(P(("dp", "mp"), None), P(("dp", "mp"), None), P(), P()),
        out_specs=(P(("dp", "mp"), None), P(("dp", "mp"), None)),
        check_vma=False,
    )
```

```python
import jax
import jax.numpy as jnp
from jax import lax
from jax.experimental import pallas as pl
from jax.experimental.pallas import tpu as pltpu
from jax.sharding import PartitionSpec as P

SHIFTS = 4
SIZES = (32, 64, 64, 32)
STARTS = (0, 32, 96, 160)
CHUNKS = len(SIZES)
FAR_DEPTH, NEAR_DEPTH = 4, 3

FAR_FIRST = 0
NEAR_OWN = 1
CORE_NEAR_OWN = 2
FAR_SECOND = 3
NEAR_FAR = 4
CORE_NEAR_FAR = 5
CORE_OWN = 6
CORE_FAR = 7


def kernel(
    log_scale_ref, bias_ref, image_ref, text_ref, total,
    own, turned, *scratch,
):
    dp_count, mp_count = lax.axis_size("dp"), lax.axis_size("mp")
    count = dp_count * mp_count
    me = lax.axis_index("dp") * mp_count + lax.axis_index("mp")
    core = lax.rem(me, 2)
    side = lax.rem(me // 2, 2)
    rows, width = image_ref.shape
    held = scratch[:CHUNKS]
    twin_held, load_sem, send_sem, recv_sem = scratch[CHUNKS:]

    def place(index):
        return (index // mp_count, lax.rem(index, mp_count))

    after = place(lax.rem(me + SHIFTS, count))
    before = place(lax.rem(me + count - SHIFTS, count))
    near = place(me + 2 - 4 * side)
    twin = place(me + 1 - 2 * core)

    loads = [
        pltpu.make_async_copy(image_ref, own.at[0], load_sem.at[0]),
        pltpu.make_async_copy(text_ref, own.at[1], load_sem.at[1]),
    ]
    for load in loads:
        load.start()

    barrier = pltpu.get_barrier_semaphore()
    for other in (after, before, near, twin):
        pl.semaphore_signal(barrier, inc=1, device_id=other, device_id_type=pl.DeviceIdType.MESH)
    pl.semaphore_wait(barrier, 4)
    for load in loads:
        load.wait()

    def remote(source, target, slot, chunk, device):
        return pltpu.make_async_remote_copy(
            src_ref=source,
            dst_ref=target,
            send_sem=send_sem.at[slot, chunk],
            recv_sem=recv_sem.at[slot, chunk],
            device_id=device,
            device_id_type=pl.DeviceIdType.MESH,
        )

    def span(chunk):
        return pl.ds(STARTS[chunk], SIZES[chunk])

    def far(kind, slot, chunk):
        device = tuple(jnp.where(kind == 0, b, a) for a, b in zip(after, before))
        return remote(own.at[kind, span(chunk)], held[chunk].at[slot], slot, chunk, device)

    first, second = side, 1 - side
    chunks = range(CHUNKS)

    def passed(source, slot, device):
        return [remote(held[i].at[source], held[i].at[slot], slot, i, device) for i in chunks]

    far_stream = [far(first, FAR_FIRST, i) for i in chunks] + [far(second, FAR_SECOND, i) for i in chunks]
    near_stream = [remote(own.at[1 - side, span(i)], held[i].at[NEAR_OWN], NEAR_OWN, i, near) for i in chunks]
    near_stream += passed(FAR_FIRST, NEAR_FAR, near)
    twin_stream = passed(NEAR_OWN, CORE_NEAR_OWN, twin) + passed(NEAR_FAR, CORE_NEAR_FAR, twin)
    core_own = [remote(own.at[1 - core, span(i)], twin_held.at[0, span(i)], CORE_OWN, i, twin) for i in chunks]
    far_slot = jnp.where(side == core, FAR_FIRST, FAR_SECOND)
    core_far = [remote(held[i].at[far_slot], twin_held.at[1, span(i)], CORE_FAR, i, twin) for i in chunks]

    for i in range(FAR_DEPTH):
        far_stream[i].start()
        if i < NEAR_DEPTH:
            near_stream[i].start()
    for copy in core_own:
        copy.start()

    scale = jnp.exp(jnp.full((1, rows), log_scale_ref[0], jnp.float32))
    offset = bias_ref[0]
    for kind in range(2):
        turned[kind] = own[kind].T

    def weights_of(block, kind):
        inner = jnp.dot(block, turned[1 - kind], preferred_element_type=jnp.float32)
        return jax.nn.sigmoid(scale * inner + offset)

    def add(block, kind):
        weights = (scale * weights_of(block, kind)).astype(jnp.bfloat16)
        total[1 - kind] += lax.dot_general(
            weights, block, (((0,), (0,)), ((), ())), preferred_element_type=jnp.float32
        )

    def add_batch(step):
        twin_stream[step].wait_recv()
        chunk, late = step % CHUNKS, step // CHUNKS
        block = held[chunk][3 * late : 3 * late + 3].reshape(3 * SIZES[chunk], width)
        add(block, second if late else first)

    row_ids = lax.broadcasted_iota(jnp.int32, (rows, rows), 0)
    col_ids = lax.broadcasted_iota(jnp.int32, (rows, rows), 1)
    target = jnp.where(row_ids == col_ids, 1.0, 0.0).astype(jnp.float32)
    own_weights = (scale * (weights_of(own[0], 0) - target)).astype(jnp.bfloat16)
    total[0] = jnp.dot(own_weights, own[1], preferred_element_type=jnp.float32)
    total[1] = lax.dot_general(own_weights, own[0], (((0,), (0,)), ((), ())), preferred_element_type=jnp.float32)

    steps = 2 * CHUNKS
    for step in range(steps):
        near_stream[step].wait_send()
        if step + NEAR_DEPTH < steps:
            near_stream[step + NEAR_DEPTH].start()
        near_stream[step].wait_recv()
        twin_stream[step].start()
        far_stream[step].wait_send()
        if step + FAR_DEPTH < steps:
            far_stream[step + FAR_DEPTH].start()
        far_stream[step].wait_recv()

        @pl.when((side == core) if step < CHUNKS else (side != core))
        def _():
            core_far[step % CHUNKS].start()

        if step == 0:
            for copy in core_own:
                copy.wait_recv()
            add(twin_held[0], core)
        else:
            add_batch(step - 1)

    early = STARTS[-1]
    for copy in core_far[:-1]:
        copy.wait_recv()
    add(twin_held[1, :early], 1 - core)
    add_batch(steps - 1)
    core_far[-1].wait_recv()
    add(twin_held[1, early:], 1 - core)

    for copies in (twin_stream, core_own, core_far):
        for copy in copies:
            copy.wait_send()


def write_out(total, image_out, text_out, store_sem):
    stores = [
        pltpu.make_async_copy(total.at[0], image_out, store_sem.at[0]),
        pltpu.make_async_copy(total.at[1], text_out, store_sem.at[1]),
    ]
    for store in stores:
        store.start()
    for store in stores:
        store.wait()


def local(image_emb, text_emb, log_scale, bias):
    rows, width = image_emb.shape
    block = jax.ShapeDtypeStruct((rows, width), jnp.float32)
    assert rows == sum(SIZES)
    in_hbm = [pltpu.with_memory_space_constraint(value, pltpu.HBM) for value in (image_emb, text_emb)]
    total = pl.pallas_call(
        kernel,
        out_shape=pltpu.VMEM((2, rows, width), jnp.float32),
        in_specs=[pl.BlockSpec(memory_space=pltpu.SMEM)] * 2 + [pl.BlockSpec(memory_space=pl.ANY)] * 2,
        out_specs=pl.BlockSpec(memory_space=pltpu.VMEM),
        scratch_shapes=[
            pltpu.VMEM((2, rows, width), jnp.bfloat16),
            pltpu.VMEM((2, width, rows), jnp.bfloat16),
            *[pltpu.VMEM((6, size, width), jnp.bfloat16) for size in SIZES],
            pltpu.VMEM((2, rows, width), jnp.bfloat16),
            pltpu.SemaphoreType.DMA((2,)),
            pltpu.SemaphoreType.DMA((8, CHUNKS)),
            pltpu.SemaphoreType.DMA((8, CHUNKS)),
        ],
        compiler_params=pltpu.CompilerParams(
            collective_id=0, has_side_effects=True, vmem_limit_bytes=32 * 1024 * 1024
        ),
        cost_estimate=pl.CostEstimate(
            flops=20 * 2 * rows * rows * width, bytes_accessed=12 * rows * width, transcendentals=9 * rows * rows
        ),
    )(log_scale, bias, *in_hbm)
    return pl.pallas_call(
        write_out,
        out_shape=(block, block),
        in_specs=[pl.BlockSpec(memory_space=pl.ANY)],
        out_specs=(pl.BlockSpec(memory_space=pl.ANY), pl.BlockSpec(memory_space=pl.ANY)),
        scratch_shapes=[pltpu.SemaphoreType.DMA((2,))],
        compiler_params=pltpu.CompilerParams(vmem_limit_bytes=1024 * 1024),
        cost_estimate=pl.CostEstimate(flops=0, bytes_accessed=16 * rows * width, transcendentals=0),
    )(total)


def solution(mesh):
    count = 1
    for axis in ("dp", "mp"):
        count *= mesh.shape[axis]
    assert mesh.shape["mp"] % 4 == 0 and count > 2 * SHIFTS
    return jax.shard_map(
        local,
        mesh=mesh,
        in_specs=(P(("dp", "mp"), None), P(("dp", "mp"), None), P(), P()),
        out_specs=(P(("dp", "mp"), None), P(("dp", "mp"), None)),
        check_vma=False,
    )
```

```python
import jax
import jax.numpy as jnp
from jax import lax
from jax.experimental import pallas as pl
from jax.experimental.pallas import tpu as pltpu
from jax.sharding import PartitionSpec as P

SHIFTS = 4
SIZES = (32, 64, 64, 32)
STARTS = (0, 32, 96, 160)
CHUNKS = len(SIZES)

FAR_FIRST = 0
NEAR_OWN = 1
CORE_NEAR_OWN = 2
FAR_SECOND = 3
NEAR_FAR = 4
CORE_NEAR_FAR = 5
CORE_OWN = 6
CORE_FAR = 7


def kernel(
    log_scale_ref, bias_ref, image_ref, text_ref, total,
    own, turned, *scratch,
):
    dp_count, mp_count = lax.axis_size("dp"), lax.axis_size("mp")
    count = dp_count * mp_count
    me = lax.axis_index("dp") * mp_count + lax.axis_index("mp")
    core = lax.rem(me, 2)
    side = lax.rem(me // 2, 2)
    rows, width = image_ref.shape
    held = scratch[:CHUNKS]
    twin_held, load_sem, send_sem, recv_sem = scratch[CHUNKS:]

    def place(index):
        return (index // mp_count, lax.rem(index, mp_count))

    after = place(lax.rem(me + SHIFTS, count))
    before = place(lax.rem(me + count - SHIFTS, count))
    near = place(me + 2 - 4 * side)
    twin = place(me + 1 - 2 * core)

    loads = [
        pltpu.make_async_copy(image_ref, own.at[0], load_sem.at[0]),
        pltpu.make_async_copy(text_ref, own.at[1], load_sem.at[1]),
    ]
    for load in loads:
        load.start()

    barrier = pltpu.get_barrier_semaphore()
    for other in (after, before, near, twin):
        pl.semaphore_signal(barrier, inc=1, device_id=other, device_id_type=pl.DeviceIdType.MESH)
    pl.semaphore_wait(barrier, 4)
    for load in loads:
        load.wait()

    def remote(source, target, slot, chunk, device):
        return pltpu.make_async_remote_copy(
            src_ref=source,
            dst_ref=target,
            send_sem=send_sem.at[slot, chunk],
            recv_sem=recv_sem.at[slot, chunk],
            device_id=device,
            device_id_type=pl.DeviceIdType.MESH,
        )

    def span(chunk):
        return pl.ds(STARTS[chunk], SIZES[chunk])

    def far(kind, slot, chunk):
        device = tuple(jnp.where(kind == 0, b, a) for a, b in zip(after, before))
        return remote(own.at[kind, span(chunk)], held[chunk].at[slot], slot, chunk, device)

    first, second = side, 1 - side
    chunks = range(CHUNKS)

    def passed(source, slot, device):
        return [remote(held[i].at[source], held[i].at[slot], slot, i, device) for i in chunks]

    far_stream = [far(first, FAR_FIRST, i) for i in chunks] + [far(second, FAR_SECOND, i) for i in chunks]
    near_stream = [remote(own.at[1 - side, span(i)], held[i].at[NEAR_OWN], NEAR_OWN, i, near) for i in chunks]
    near_stream += passed(FAR_FIRST, NEAR_FAR, near)
    twin_stream = passed(NEAR_OWN, CORE_NEAR_OWN, twin) + passed(NEAR_FAR, CORE_NEAR_FAR, twin)
    core_own = [remote(own.at[1 - core, span(i)], twin_held.at[0, span(i)], CORE_OWN, i, twin) for i in chunks]
    far_slot = jnp.where(side == core, FAR_FIRST, FAR_SECOND)
    core_far = [remote(held[i].at[far_slot], twin_held.at[1, span(i)], CORE_FAR, i, twin) for i in chunks]

    far_first, far_second = far_stream[:CHUNKS], far_stream[CHUNKS:]
    near_own, near_far = near_stream[:CHUNKS], near_stream[CHUNKS:]

    def start(*groups):
        for group in groups:
            for copy in group:
                copy.start()

    @pl.when(core == 0)
    def _():
        start(far_first, core_own, near_own)

    @pl.when(core != 0)
    def _():
        start(near_own, core_own, far_first)

    scale = jnp.exp(jnp.full((1, rows), log_scale_ref[0], jnp.float32))
    offset = bias_ref[0]
    for kind in range(2):
        turned[kind] = own[kind].T

    def weights_of(block, kind):
        inner = jnp.dot(block, turned[1 - kind], preferred_element_type=jnp.float32)
        return jax.nn.sigmoid(scale * inner + offset)

    def add(block, kind):
        weights = (scale * weights_of(block, kind)).astype(jnp.bfloat16)
        total[1 - kind] += lax.dot_general(
            weights, block, (((0,), (0,)), ((), ())), preferred_element_type=jnp.float32
        )

    def add_batch(step):
        twin_stream[step].wait_recv()
        chunk, late = step % CHUNKS, step // CHUNKS
        block = held[chunk][3 * late : 3 * late + 3].reshape(3 * SIZES[chunk], width)
        add(block, second if late else first)

    row_ids = lax.broadcasted_iota(jnp.int32, (rows, rows), 0)
    col_ids = lax.broadcasted_iota(jnp.int32, (rows, rows), 1)
    target = jnp.where(row_ids == col_ids, 1.0, 0.0).astype(jnp.float32)
    own_weights = (scale * (weights_of(own[0], 0) - target)).astype(jnp.bfloat16)
    total[0] = jnp.dot(own_weights, own[1], preferred_element_type=jnp.float32)
    total[1] = lax.dot_general(own_weights, own[0], (((0,), (0,)), ((), ())), preferred_element_type=jnp.float32)

    for copy in core_own:
        copy.wait_recv()
    add(twin_held[0], core)

    def take_far(second_too):
        for i in chunks:
            far_first[i].wait_recv()
            near_far[i].start()

            @pl.when(side == core)
            def _():
                core_far[i].start()

        if second_too:
            start(far_second)

    def take_near():
        for i in chunks:
            near_own[i].wait_recv()
            twin_stream[i].start()

    @pl.when(core == 0)
    def _():
        take_far(True)
        take_near()

    @pl.when(core != 0)
    def _():
        take_near()
        start(far_second)
        take_far(False)

    for i in chunks:
        add_batch(i)
    for i in chunks:
        near_far[i].wait_recv()
        twin_stream[CHUNKS + i].start()
        far_second[i].wait_recv()

        @pl.when(side != core)
        def _():
            core_far[i].start()

        if i > 0:
            add_batch(CHUNKS + i - 1)

    early = STARTS[-1]
    for copy in core_far[:-1]:
        copy.wait_recv()
    add(twin_held[1, :early], 1 - core)
    add_batch(2 * CHUNKS - 1)
    core_far[-1].wait_recv()
    add(twin_held[1, early:], 1 - core)

    for copies in (far_stream, near_stream, twin_stream, core_own, core_far):
        for copy in copies:
            copy.wait_send()


def write_out(total, image_out, text_out, store_sem):
    stores = [
        pltpu.make_async_copy(total.at[0], image_out, store_sem.at[0]),
        pltpu.make_async_copy(total.at[1], text_out, store_sem.at[1]),
    ]
    for store in stores:
        store.start()
    for store in stores:
        store.wait()


def local(image_emb, text_emb, log_scale, bias):
    rows, width = image_emb.shape
    block = jax.ShapeDtypeStruct((rows, width), jnp.float32)
    assert rows == sum(SIZES)
    in_hbm = [pltpu.with_memory_space_constraint(value, pltpu.HBM) for value in (image_emb, text_emb)]
    total = pl.pallas_call(
        kernel,
        out_shape=pltpu.VMEM((2, rows, width), jnp.float32),
        in_specs=[pl.BlockSpec(memory_space=pltpu.SMEM)] * 2 + [pl.BlockSpec(memory_space=pl.ANY)] * 2,
        out_specs=pl.BlockSpec(memory_space=pltpu.VMEM),
        scratch_shapes=[
            pltpu.VMEM((2, rows, width), jnp.bfloat16),
            pltpu.VMEM((2, width, rows), jnp.bfloat16),
            *[pltpu.VMEM((6, size, width), jnp.bfloat16) for size in SIZES],
            pltpu.VMEM((2, rows, width), jnp.bfloat16),
            pltpu.SemaphoreType.DMA((2,)),
            pltpu.SemaphoreType.DMA((8, CHUNKS)),
            pltpu.SemaphoreType.DMA((8, CHUNKS)),
        ],
        compiler_params=pltpu.CompilerParams(
            collective_id=0, has_side_effects=True, vmem_limit_bytes=32 * 1024 * 1024
        ),
        cost_estimate=pl.CostEstimate(
            flops=20 * 2 * rows * rows * width, bytes_accessed=12 * rows * width, transcendentals=9 * rows * rows
        ),
    )(log_scale, bias, *in_hbm)
    return pl.pallas_call(
        write_out,
        out_shape=(block, block),
        in_specs=[pl.BlockSpec(memory_space=pl.ANY)],
        out_specs=(pl.BlockSpec(memory_space=pl.ANY), pl.BlockSpec(memory_space=pl.ANY)),
        scratch_shapes=[pltpu.SemaphoreType.DMA((2,))],
        compiler_params=pltpu.CompilerParams(vmem_limit_bytes=1024 * 1024),
        cost_estimate=pl.CostEstimate(flops=0, bytes_accessed=16 * rows * width, transcendentals=0),
    )(total)


def solution(mesh):
    count = 1
    for axis in ("dp", "mp"):
        count *= mesh.shape[axis]
    assert mesh.shape["mp"] % 4 == 0 and count > 2 * SHIFTS
    return jax.shard_map(
        local,
        mesh=mesh,
        in_specs=(P(("dp", "mp"), None), P(("dp", "mp"), None), P(), P()),
        out_specs=(P(("dp", "mp"), None), P(("dp", "mp"), None)),
        check_vma=False,
    )
```

```python
import jax
import jax.numpy as jnp
from jax import lax
from jax.experimental import pallas as pl
from jax.experimental.pallas import tpu as pltpu
from jax.sharding import PartitionSpec as P

SHIFTS = 4
SIZES = (32, 64, 64, 32)
STARTS = (0, 32, 96, 160)
CHUNKS = len(SIZES)

FAR_FIRST = 0
NEAR_OWN = 1
CORE_NEAR_OWN = 2
FAR_SECOND = 3
NEAR_FAR = 4
CORE_NEAR_FAR = 5
CORE_OWN = 6
CORE_FAR = 7


def kernel(
    log_scale_ref, bias_ref, image_ref, text_ref, total,
    own, turned, *scratch,
):
    dp_count, mp_count = lax.axis_size("dp"), lax.axis_size("mp")
    count = dp_count * mp_count
    me = lax.axis_index("dp") * mp_count + lax.axis_index("mp")
    core = lax.rem(me, 2)
    side = lax.rem(me // 2, 2)
    rows, width = image_ref.shape
    held = scratch[:CHUNKS]
    twin_held, load_sem, send_sem, recv_sem = scratch[CHUNKS:]

    def place(index):
        return (index // mp_count, lax.rem(index, mp_count))

    after = place(lax.rem(me + SHIFTS, count))
    before = place(lax.rem(me + count - SHIFTS, count))
    near = place(me + 2 - 4 * side)
    twin = place(me + 1 - 2 * core)

    loads = [
        pltpu.make_async_copy(image_ref, own.at[0], load_sem.at[0]),
        pltpu.make_async_copy(text_ref, own.at[1], load_sem.at[1]),
    ]
    for load in loads:
        load.start()

    barrier = pltpu.get_barrier_semaphore()
    for other in (after, before, near, twin):
        pl.semaphore_signal(barrier, inc=1, device_id=other, device_id_type=pl.DeviceIdType.MESH)
    pl.semaphore_wait(barrier, 4)
    for load in loads:
        load.wait()

    def remote(source, target, slot, chunk, device):
        return pltpu.make_async_remote_copy(
            src_ref=source,
            dst_ref=target,
            send_sem=send_sem.at[slot, chunk],
            recv_sem=recv_sem.at[slot, chunk],
            device_id=device,
            device_id_type=pl.DeviceIdType.MESH,
        )

    def span(chunk):
        return pl.ds(STARTS[chunk], SIZES[chunk])

    def far(kind, slot, chunk):
        device = tuple(jnp.where(kind == 0, b, a) for a, b in zip(after, before))
        return remote(own.at[kind, span(chunk)], held[chunk].at[slot], slot, chunk, device)

    first, second = side, 1 - side
    chunks = range(CHUNKS)

    def passed(source, slot, device):
        return [remote(held[i].at[source], held[i].at[slot], slot, i, device) for i in chunks]

    far_stream = [far(first, FAR_FIRST, i) for i in chunks] + [far(second, FAR_SECOND, i) for i in chunks]
    near_stream = [remote(own.at[1 - side, span(i)], held[i].at[NEAR_OWN], NEAR_OWN, i, near) for i in chunks]
    near_stream += passed(FAR_FIRST, NEAR_FAR, near)
    twin_stream = passed(NEAR_OWN, CORE_NEAR_OWN, twin) + passed(NEAR_FAR, CORE_NEAR_FAR, twin)
    core_own = [remote(own.at[1 - core, span(i)], twin_held.at[0, span(i)], CORE_OWN, i, twin) for i in chunks]
    far_slot = jnp.where(side == core, FAR_FIRST, FAR_SECOND)
    core_far = [remote(held[i].at[far_slot], twin_held.at[1, span(i)], CORE_FAR, i, twin) for i in chunks]

    far_first, far_second = far_stream[:CHUNKS], far_stream[CHUNKS:]
    near_own, near_far = near_stream[:CHUNKS], near_stream[CHUNKS:]

    def start(*groups):
        for group in groups:
            for copy in group:
                copy.start()

    second_wraps = jnp.logical_or(
        jnp.logical_and(second == 0, me < SHIFTS), jnp.logical_and(second == 1, me >= count - SHIFTS)
    )

    @pl.when(core == 0)
    def _():
        start(far_first, core_own, near_own)

        @pl.when(second_wraps)
        def _():
            start(far_second)

    @pl.when(core != 0)
    def _():
        start(near_own, core_own, far_first, far_second)

    scale = jnp.exp(jnp.full((1, rows), log_scale_ref[0], jnp.float32))
    offset = bias_ref[0]
    for kind in range(2):
        turned[kind] = own[kind].T

    def weights_of(block, kind):
        inner = jnp.dot(block, turned[1 - kind], preferred_element_type=jnp.float32)
        return jax.nn.sigmoid(scale * inner + offset)

    def add(block, kind):
        weights = (scale * weights_of(block, kind)).astype(jnp.bfloat16)
        total[1 - kind] += lax.dot_general(
            weights, block, (((0,), (0,)), ((), ())), preferred_element_type=jnp.float32
        )

    def add_batch(step):
        twin_stream[step].wait_recv()
        chunk, late = step % CHUNKS, step // CHUNKS
        block = held[chunk][3 * late : 3 * late + 3].reshape(3 * SIZES[chunk], width)
        add(block, second if late else first)

    row_ids = lax.broadcasted_iota(jnp.int32, (rows, rows), 0)
    col_ids = lax.broadcasted_iota(jnp.int32, (rows, rows), 1)
    target = jnp.where(row_ids == col_ids, 1.0, 0.0).astype(jnp.float32)
    own_weights = (scale * (weights_of(own[0], 0) - target)).astype(jnp.bfloat16)
    total[0] = jnp.dot(own_weights, own[1], preferred_element_type=jnp.float32)
    total[1] = lax.dot_general(own_weights, own[0], (((0,), (0,)), ((), ())), preferred_element_type=jnp.float32)

    for copy in core_own:
        copy.wait_recv()
    add(twin_held[0], core)

    def take_far():
        for i in chunks:
            far_first[i].wait_recv()
            near_far[i].start()

            @pl.when(side == core)
            def _():
                core_far[i].start()

    def take_near():
        for i in chunks:
            near_own[i].wait_recv()
            twin_stream[i].start()

    @pl.when(core == 0)
    def _():
        take_far()

        @pl.when(jnp.logical_not(second_wraps))
        def _():
            start(far_second)

        take_near()

    @pl.when(core != 0)
    def _():
        take_near()
        take_far()

    for i in chunks:
        add_batch(i)
    for i in chunks:
        near_far[i].wait_recv()
        twin_stream[CHUNKS + i].start()
        far_second[i].wait_recv()

        @pl.when(side != core)
        def _():
            core_far[i].start()

        if i > 0:
            add_batch(CHUNKS + i - 1)

    early = STARTS[-1]
    for copy in core_far[:-1]:
        copy.wait_recv()
    add(twin_held[1, :early], 1 - core)
    add_batch(2 * CHUNKS - 1)
    core_far[-1].wait_recv()
    add(twin_held[1, early:], 1 - core)

    for copies in (far_stream, near_stream, twin_stream, core_own, core_far):
        for copy in copies:
            copy.wait_send()


def write_out(total, image_out, text_out, store_sem):
    stores = [
        pltpu.make_async_copy(total.at[0], image_out, store_sem.at[0]),
        pltpu.make_async_copy(total.at[1], text_out, store_sem.at[1]),
    ]
    for store in stores:
        store.start()
    for store in stores:
        store.wait()


def local(image_emb, text_emb, log_scale, bias):
    rows, width = image_emb.shape
    block = jax.ShapeDtypeStruct((rows, width), jnp.float32)
    assert rows == sum(SIZES)
    in_hbm = [pltpu.with_memory_space_constraint(value, pltpu.HBM) for value in (image_emb, text_emb)]
    total = pl.pallas_call(
        kernel,
        out_shape=pltpu.VMEM((2, rows, width), jnp.float32),
        in_specs=[pl.BlockSpec(memory_space=pltpu.SMEM)] * 2 + [pl.BlockSpec(memory_space=pl.ANY)] * 2,
        out_specs=pl.BlockSpec(memory_space=pltpu.VMEM),
        scratch_shapes=[
            pltpu.VMEM((2, rows, width), jnp.bfloat16),
            pltpu.VMEM((2, width, rows), jnp.bfloat16),
            *[pltpu.VMEM((6, size, width), jnp.bfloat16) for size in SIZES],
            pltpu.VMEM((2, rows, width), jnp.bfloat16),
            pltpu.SemaphoreType.DMA((2,)),
            pltpu.SemaphoreType.DMA((8, CHUNKS)),
            pltpu.SemaphoreType.DMA((8, CHUNKS)),
        ],
        compiler_params=pltpu.CompilerParams(
            collective_id=0, has_side_effects=True, vmem_limit_bytes=32 * 1024 * 1024
        ),
        cost_estimate=pl.CostEstimate(
            flops=20 * 2 * rows * rows * width, bytes_accessed=12 * rows * width, transcendentals=9 * rows * rows
        ),
    )(log_scale, bias, *in_hbm)
    return pl.pallas_call(
        write_out,
        out_shape=(block, block),
        in_specs=[pl.BlockSpec(memory_space=pl.ANY)],
        out_specs=(pl.BlockSpec(memory_space=pl.ANY), pl.BlockSpec(memory_space=pl.ANY)),
        scratch_shapes=[pltpu.SemaphoreType.DMA((2,))],
        compiler_params=pltpu.CompilerParams(vmem_limit_bytes=1024 * 1024),
        cost_estimate=pl.CostEstimate(flops=0, bytes_accessed=16 * rows * width, transcendentals=0),
    )(total)


def solution(mesh):
    count = 1
    for axis in ("dp", "mp"):
        count *= mesh.shape[axis]
    assert mesh.shape["mp"] % 4 == 0 and count > 2 * SHIFTS
    return jax.shard_map(
        local,
        mesh=mesh,
        in_specs=(P(("dp", "mp"), None), P(("dp", "mp"), None), P(), P()),
        out_specs=(P(("dp", "mp"), None), P(("dp", "mp"), None)),
        check_vma=False,
    )
```

```python
import jax
import jax.numpy as jnp
from jax import lax
from jax.experimental import pallas as pl
from jax.experimental.pallas import tpu as pltpu
from jax.sharding import PartitionSpec as P

SHIFTS = 4
SIZES = (32, 64, 64, 32)
STARTS = (0, 32, 96, 160)
CHUNKS = len(SIZES)

FAR_FIRST = 0
NEAR_OWN = 1
CORE_NEAR_OWN = 2
FAR_SECOND = 3
NEAR_FAR = 4
CORE_NEAR_FAR = 5
CORE_OWN = 6
CORE_FAR = 7


def kernel(
    log_scale_ref, bias_ref, image_ref, text_ref, total,
    own, turned, *scratch,
):
    dp_count, mp_count = lax.axis_size("dp"), lax.axis_size("mp")
    count = dp_count * mp_count
    me = lax.axis_index("dp") * mp_count + lax.axis_index("mp")
    core = lax.rem(me, 2)
    side = lax.rem(me // 2, 2)
    rows, width = image_ref.shape
    held = scratch[:CHUNKS]
    twin_held, load_sem, send_sem, recv_sem = scratch[CHUNKS:]

    def place(index):
        return (index // mp_count, lax.rem(index, mp_count))

    after = place(lax.rem(me + SHIFTS, count))
    before = place(lax.rem(me + count - SHIFTS, count))
    near = place(me + 2 - 4 * side)
    twin = place(me + 1 - 2 * core)

    loads = [
        pltpu.make_async_copy(image_ref, own.at[0], load_sem.at[0]),
        pltpu.make_async_copy(text_ref, own.at[1], load_sem.at[1]),
    ]
    for load in loads:
        load.start()

    barrier = pltpu.get_barrier_semaphore()
    for other in (after, before, near, twin):
        pl.semaphore_signal(barrier, inc=1, device_id=other, device_id_type=pl.DeviceIdType.MESH)
    pl.semaphore_wait(barrier, 4)
    for load in loads:
        load.wait()

    def remote(source, target, slot, chunk, device):
        return pltpu.make_async_remote_copy(
            src_ref=source,
            dst_ref=target,
            send_sem=send_sem.at[slot, chunk],
            recv_sem=recv_sem.at[slot, chunk],
            device_id=device,
            device_id_type=pl.DeviceIdType.MESH,
        )

    def span(chunk):
        return pl.ds(STARTS[chunk], SIZES[chunk])

    def far(kind, slot, chunk):
        device = tuple(jnp.where(kind == 0, b, a) for a, b in zip(after, before))
        return remote(own.at[kind, span(chunk)], held[chunk].at[slot], slot, chunk, device)

    first, second = side, 1 - side
    chunks = range(CHUNKS)

    def passed(source, slot, device):
        return [remote(held[i].at[source], held[i].at[slot], slot, i, device) for i in chunks]

    far_stream = [far(first, FAR_FIRST, i) for i in chunks] + [far(second, FAR_SECOND, i) for i in chunks]
    near_stream = [remote(own.at[1 - side, span(i)], held[i].at[NEAR_OWN], NEAR_OWN, i, near) for i in chunks]
    near_stream += passed(FAR_FIRST, NEAR_FAR, near)
    twin_stream = passed(NEAR_OWN, CORE_NEAR_OWN, twin) + passed(NEAR_FAR, CORE_NEAR_FAR, twin)
    core_own = [remote(own.at[1 - core, span(i)], twin_held.at[0, span(i)], CORE_OWN, i, twin) for i in chunks]
    far_slot = jnp.where(side == core, FAR_FIRST, FAR_SECOND)
    core_far = [remote(held[i].at[far_slot], twin_held.at[1, span(i)], CORE_FAR, i, twin) for i in chunks]

    far_first, far_second = far_stream[:CHUNKS], far_stream[CHUNKS:]
    near_own, near_far = near_stream[:CHUNKS], near_stream[CHUNKS:]

    def start(*groups):
        for group in groups:
            for copy in group:
                copy.start()

    second_wraps = jnp.logical_or(
        jnp.logical_and(second == 0, me < SHIFTS), jnp.logical_and(second == 1, me >= count - SHIFTS)
    )

    @pl.when(core == 0)
    def _():
        start(far_first, core_own, near_own)

    @pl.when(core != 0)
    def _():
        start(near_own, core_own, far_first)

    scale = jnp.exp(jnp.full((1, rows), log_scale_ref[0], jnp.float32))
    offset = bias_ref[0]
    for kind in range(2):
        turned[kind] = own[kind].T

    def weights_of(block, kind):
        inner = jnp.dot(block, turned[1 - kind], preferred_element_type=jnp.float32)
        return jax.nn.sigmoid(scale * inner + offset)

    def add(block, kind):
        weights = (scale * weights_of(block, kind)).astype(jnp.bfloat16)
        total[1 - kind] += lax.dot_general(
            weights, block, (((0,), (0,)), ((), ())), preferred_element_type=jnp.float32
        )

    def add_batch(step):
        twin_stream[step].wait_recv()
        chunk, late = step % CHUNKS, step // CHUNKS
        block = held[chunk][3 * late : 3 * late + 3].reshape(3 * SIZES[chunk], width)
        add(block, second if late else first)

    row_ids = lax.broadcasted_iota(jnp.int32, (rows, rows), 0)
    col_ids = lax.broadcasted_iota(jnp.int32, (rows, rows), 1)
    target = jnp.where(row_ids == col_ids, 1.0, 0.0).astype(jnp.float32)
    own_weights = (scale * (weights_of(own[0], 0) - target)).astype(jnp.bfloat16)
    total[0] = jnp.dot(own_weights, own[1], preferred_element_type=jnp.float32)
    total[1] = lax.dot_general(own_weights, own[0], (((0,), (0,)), ((), ())), preferred_element_type=jnp.float32)

    for copy in core_own:
        copy.wait_recv()
    add(twin_held[0], core)

    def take_far():
        for i in chunks:
            far_first[i].wait_recv()
            near_far[i].start()

            @pl.when(side == core)
            def _():
                core_far[i].start()

    def take_near():
        for i in chunks:
            near_own[i].wait_recv()
            twin_stream[i].start()

    @pl.when(core == 0)
    def _():
        @pl.when(second_wraps)
        def _():
            for copy in far_first:
                copy.wait_send()
            start(far_second)

        take_far()

        @pl.when(jnp.logical_not(second_wraps))
        def _():
            start(far_second)

        take_near()

    @pl.when(core != 0)
    def _():
        take_near()
        start(far_second)
        take_far()

    for i in chunks:
        add_batch(i)
    early = STARTS[-1]
    for i in chunks:
        if i + 1 == CHUNKS:
            for copy in core_far[:-1]:
                copy.wait_recv()
            add(twin_held[1, :early], 1 - core)
        near_far[i].wait_recv()
        twin_stream[CHUNKS + i].start()
        far_second[i].wait_recv()

        @pl.when(side != core)
        def _():
            core_far[i].start()

        if i > 0:
            add_batch(CHUNKS + i - 1)

    add_batch(2 * CHUNKS - 1)
    core_far[-1].wait_recv()
    add(twin_held[1, early:], 1 - core)

    @pl.when(jnp.logical_not(jnp.logical_and(core == 0, second_wraps)))
    def _():
        for copy in far_first:
            copy.wait_send()

    for copies in (far_second, near_stream, twin_stream, core_own, core_far):
        for copy in copies:
            copy.wait_send()


def write_out(total, image_out, text_out, store_sem):
    stores = [
        pltpu.make_async_copy(total.at[0], image_out, store_sem.at[0]),
        pltpu.make_async_copy(total.at[1], text_out, store_sem.at[1]),
    ]
    for store in stores:
        store.start()
    for store in stores:
        store.wait()


def local(image_emb, text_emb, log_scale, bias):
    rows, width = image_emb.shape
    block = jax.ShapeDtypeStruct((rows, width), jnp.float32)
    assert rows == sum(SIZES)
    in_hbm = [pltpu.with_memory_space_constraint(value, pltpu.HBM) for value in (image_emb, text_emb)]
    total = pl.pallas_call(
        kernel,
        out_shape=pltpu.VMEM((2, rows, width), jnp.float32),
        in_specs=[pl.BlockSpec(memory_space=pltpu.SMEM)] * 2 + [pl.BlockSpec(memory_space=pl.ANY)] * 2,
        out_specs=pl.BlockSpec(memory_space=pltpu.VMEM),
        scratch_shapes=[
            pltpu.VMEM((2, rows, width), jnp.bfloat16),
            pltpu.VMEM((2, width, rows), jnp.bfloat16),
            *[pltpu.VMEM((6, size, width), jnp.bfloat16) for size in SIZES],
            pltpu.VMEM((2, rows, width), jnp.bfloat16),
            pltpu.SemaphoreType.DMA((2,)),
            pltpu.SemaphoreType.DMA((8, CHUNKS)),
            pltpu.SemaphoreType.DMA((8, CHUNKS)),
        ],
        compiler_params=pltpu.CompilerParams(
            collective_id=0, has_side_effects=True, vmem_limit_bytes=32 * 1024 * 1024
        ),
        cost_estimate=pl.CostEstimate(
            flops=20 * 2 * rows * rows * width, bytes_accessed=12 * rows * width, transcendentals=9 * rows * rows
        ),
    )(log_scale, bias, *in_hbm)
    return pl.pallas_call(
        write_out,
        out_shape=(block, block),
        in_specs=[pl.BlockSpec(memory_space=pl.ANY)],
        out_specs=(pl.BlockSpec(memory_space=pl.ANY), pl.BlockSpec(memory_space=pl.ANY)),
        scratch_shapes=[pltpu.SemaphoreType.DMA((2,))],
        compiler_params=pltpu.CompilerParams(vmem_limit_bytes=1024 * 1024),
        cost_estimate=pl.CostEstimate(flops=0, bytes_accessed=16 * rows * width, transcendentals=0),
    )(total)


def solution(mesh):
    count = 1
    for axis in ("dp", "mp"):
        count *= mesh.shape[axis]
    assert mesh.shape["mp"] % 4 == 0 and count > 2 * SHIFTS
    return jax.shard_map(
        local,
        mesh=mesh,
        in_specs=(P(("dp", "mp"), None), P(("dp", "mp"), None), P(), P()),
        out_specs=(P(("dp", "mp"), None), P(("dp", "mp"), None)),
        check_vma=False,
    )
```

```python
import jax
import jax.numpy as jnp
from jax import lax
from jax.experimental import pallas as pl
from jax.experimental.pallas import tpu as pltpu
from jax.sharding import PartitionSpec as P

SHIFTS = 4
SIZES = (48, 48, 48, 48)
STARTS = (0, 48, 96, 144)
CHUNKS = len(SIZES)

FAR_FIRST = 0
NEAR_OWN = 1
CORE_NEAR_OWN = 2
FAR_SECOND = 3
NEAR_FAR = 4
CORE_NEAR_FAR = 5
CORE_OWN = 6
CORE_FAR = 7


def kernel(
    log_scale_ref, bias_ref, image_ref, text_ref, total,
    own, turned, *scratch,
):
    dp_count, mp_count = lax.axis_size("dp"), lax.axis_size("mp")
    count = dp_count * mp_count
    me = lax.axis_index("dp") * mp_count + lax.axis_index("mp")
    core = lax.rem(me, 2)
    side = lax.rem(me // 2, 2)
    rows, width = image_ref.shape
    held = scratch[:CHUNKS]
    twin_held, load_sem, send_sem, recv_sem = scratch[CHUNKS:]

    def place(index):
        return (index // mp_count, lax.rem(index, mp_count))

    after = place(lax.rem(me + SHIFTS, count))
    before = place(lax.rem(me + count - SHIFTS, count))
    near = place(me + 2 - 4 * side)
    twin = place(me + 1 - 2 * core)

    loads = [
        pltpu.make_async_copy(image_ref, own.at[0], load_sem.at[0]),
        pltpu.make_async_copy(text_ref, own.at[1], load_sem.at[1]),
    ]
    for load in loads:
        load.start()

    barrier = pltpu.get_barrier_semaphore()
    for other in (after, before, near, twin):
        pl.semaphore_signal(barrier, inc=1, device_id=other, device_id_type=pl.DeviceIdType.MESH)
    pl.semaphore_wait(barrier, 4)
    for load in loads:
        load.wait()

    def remote(source, target, slot, chunk, device):
        return pltpu.make_async_remote_copy(
            src_ref=source,
            dst_ref=target,
            send_sem=send_sem.at[slot, chunk],
            recv_sem=recv_sem.at[slot, chunk],
            device_id=device,
            device_id_type=pl.DeviceIdType.MESH,
        )

    def span(chunk):
        return pl.ds(STARTS[chunk], SIZES[chunk])

    def far(kind, slot, chunk):
        device = tuple(jnp.where(kind == 0, b, a) for a, b in zip(after, before))
        return remote(own.at[kind, span(chunk)], held[chunk].at[slot], slot, chunk, device)

    first, second = side, 1 - side
    chunks = range(CHUNKS)

    def passed(source, slot, device):
        return [remote(held[i].at[source], held[i].at[slot], slot, i, device) for i in chunks]

    far_stream = [far(first, FAR_FIRST, i) for i in chunks] + [far(second, FAR_SECOND, i) for i in chunks]
    near_stream = [remote(own.at[1 - side, span(i)], held[i].at[NEAR_OWN], NEAR_OWN, i, near) for i in chunks]
    near_stream += passed(FAR_FIRST, NEAR_FAR, near)
    twin_stream = passed(NEAR_OWN, CORE_NEAR_OWN, twin) + passed(NEAR_FAR, CORE_NEAR_FAR, twin)
    core_own = [remote(own.at[1 - core, span(i)], twin_held.at[0, span(i)], CORE_OWN, i, twin) for i in chunks]
    far_slot = jnp.where(side == core, FAR_FIRST, FAR_SECOND)
    core_far = [remote(held[i].at[far_slot], twin_held.at[1, span(i)], CORE_FAR, i, twin) for i in chunks]

    far_first, far_second = far_stream[:CHUNKS], far_stream[CHUNKS:]
    near_own, near_far = near_stream[:CHUNKS], near_stream[CHUNKS:]

    for i in chunks:
        far_first[i].start()
        near_own[i].start()
    for i in chunks:
        far_second[i].start()
        core_own[i].start()

    scale = jnp.exp(jnp.full((1, rows), log_scale_ref[0], jnp.float32))
    offset = bias_ref[0]
    for kind in range(2):
        turned[kind] = own[kind].T

    def weights_of(block, kind):
        inner = jnp.dot(block, turned[1 - kind], preferred_element_type=jnp.float32)
        return jax.nn.sigmoid(scale * inner + offset)

    def add(block, kind):
        weights = (scale * weights_of(block, kind)).astype(jnp.bfloat16)
        total[1 - kind] += lax.dot_general(
            weights, block, (((0,), (0,)), ((), ())), preferred_element_type=jnp.float32
        )

    def add_batch(step):
        twin_stream[step].wait_recv()
        chunk, late = step % CHUNKS, step // CHUNKS
        block = held[chunk][3 * late : 3 * late + 3].reshape(3 * SIZES[chunk], width)
        add(block, second if late else first)

    row_ids = lax.broadcasted_iota(jnp.int32, (rows, rows), 0)
    col_ids = lax.broadcasted_iota(jnp.int32, (rows, rows), 1)
    target = jnp.where(row_ids == col_ids, 1.0, 0.0).astype(jnp.float32)
    own_weights = (scale * (weights_of(own[0], 0) - target)).astype(jnp.bfloat16)
    total[0] = jnp.dot(own_weights, own[1], preferred_element_type=jnp.float32)
    total[1] = lax.dot_general(own_weights, own[0], (((0,), (0,)), ((), ())), preferred_element_type=jnp.float32)

    for copy in core_own:
        copy.wait_recv()
    add(twin_held[0], core)

    for i in chunks:
        far_first[i].wait_recv()
        near_far[i].start()

        @pl.when(side == core)
        def _():
            core_far[i].start()

    for i in chunks:
        near_own[i].wait_recv()
        twin_stream[i].start()

    for i in chunks:
        add_batch(i)
    for i in chunks:
        near_far[i].wait_recv()
        twin_stream[CHUNKS + i].start()
        far_second[i].wait_recv()

        @pl.when(side != core)
        def _():
            core_far[i].start()

        if i > 0:
            add_batch(CHUNKS + i - 1)

    for copy in core_far:
        copy.wait_recv()
    add(twin_held[1], 1 - core)
    add_batch(2 * CHUNKS - 1)

    for copies in (far_stream, near_stream, twin_stream, core_own, core_far):
        for copy in copies:
            copy.wait_send()


def write_out(total, image_out, text_out, store_sem):
    stores = [
        pltpu.make_async_copy(total.at[0], image_out, store_sem.at[0]),
        pltpu.make_async_copy(total.at[1], text_out, store_sem.at[1]),
    ]
    for store in stores:
        store.start()
    for store in stores:
        store.wait()


def local(image_emb, text_emb, log_scale, bias):
    rows, width = image_emb.shape
    block = jax.ShapeDtypeStruct((rows, width), jnp.float32)
    assert rows == sum(SIZES)
    in_hbm = [pltpu.with_memory_space_constraint(value, pltpu.HBM) for value in (image_emb, text_emb)]
    total = pl.pallas_call(
        kernel,
        out_shape=pltpu.VMEM((2, rows, width), jnp.float32),
        in_specs=[pl.BlockSpec(memory_space=pltpu.SMEM)] * 2 + [pl.BlockSpec(memory_space=pl.ANY)] * 2,
        out_specs=pl.BlockSpec(memory_space=pltpu.VMEM),
        scratch_shapes=[
            pltpu.VMEM((2, rows, width), jnp.bfloat16),
            pltpu.VMEM((2, width, rows), jnp.bfloat16),
            *[pltpu.VMEM((6, size, width), jnp.bfloat16) for size in SIZES],
            pltpu.VMEM((2, rows, width), jnp.bfloat16),
            pltpu.SemaphoreType.DMA((2,)),
            pltpu.SemaphoreType.DMA((8, CHUNKS)),
            pltpu.SemaphoreType.DMA((8, CHUNKS)),
        ],
        compiler_params=pltpu.CompilerParams(
            collective_id=0, has_side_effects=True, vmem_limit_bytes=32 * 1024 * 1024
        ),
        cost_estimate=pl.CostEstimate(
            flops=20 * 2 * rows * rows * width, bytes_accessed=12 * rows * width, transcendentals=9 * rows * rows
        ),
    )(log_scale, bias, *in_hbm)
    return pl.pallas_call(
        write_out,
        out_shape=(block, block),
        in_specs=[pl.BlockSpec(memory_space=pl.ANY)],
        out_specs=(pl.BlockSpec(memory_space=pl.ANY), pl.BlockSpec(memory_space=pl.ANY)),
        scratch_shapes=[pltpu.SemaphoreType.DMA((2,))],
        compiler_params=pltpu.CompilerParams(vmem_limit_bytes=1024 * 1024),
        cost_estimate=pl.CostEstimate(flops=0, bytes_accessed=16 * rows * width, transcendentals=0),
    )(total)


def solution(mesh):
    count = 1
    for axis in ("dp", "mp"):
        count *= mesh.shape[axis]
    assert mesh.shape["mp"] % 4 == 0 and count > 2 * SHIFTS
    return jax.shard_map(
        local,
        mesh=mesh,
        in_specs=(P(("dp", "mp"), None), P(("dp", "mp"), None), P(), P()),
        out_specs=(P(("dp", "mp"), None), P(("dp", "mp"), None)),
        check_vma=False,
    )
```

```python
import jax
import jax.numpy as jnp
from jax import lax
from jax.experimental import pallas as pl
from jax.experimental.pallas import tpu as pltpu
from jax.sharding import PartitionSpec as P

SHIFTS = 4
SIZES = (48, 48, 48, 48)
STARTS = (0, 48, 96, 144)
CHUNKS = len(SIZES)

FAR_FIRST = 0
NEAR_OWN = 1
CORE_NEAR_OWN = 2
FAR_SECOND = 3
NEAR_FAR = 4
CORE_NEAR_FAR = 5
CORE_OWN = 6
CORE_FAR = 7


def kernel(
    log_scale_ref, bias_ref, image_ref, text_ref, total,
    own, turned, *scratch,
):
    dp_count, mp_count = lax.axis_size("dp"), lax.axis_size("mp")
    count = dp_count * mp_count
    me = lax.axis_index("dp") * mp_count + lax.axis_index("mp")
    core = lax.rem(me, 2)
    side = lax.rem(me // 2, 2)
    rows, width = image_ref.shape
    held = scratch[:CHUNKS]
    twin_held, load_sem, send_sem, recv_sem = scratch[CHUNKS:]

    def place(index):
        return (index // mp_count, lax.rem(index, mp_count))

    after = place(lax.rem(me + SHIFTS, count))
    before = place(lax.rem(me + count - SHIFTS, count))
    near = place(me + 2 - 4 * side)
    twin = place(me + 1 - 2 * core)

    loads = [
        pltpu.make_async_copy(image_ref, own.at[0], load_sem.at[0]),
        pltpu.make_async_copy(text_ref, own.at[1], load_sem.at[1]),
    ]
    for load in loads:
        load.start()

    barrier = pltpu.get_barrier_semaphore()
    for other in (after, before, near, twin):
        pl.semaphore_signal(barrier, inc=1, device_id=other, device_id_type=pl.DeviceIdType.MESH)
    pl.semaphore_wait(barrier, 4)
    for load in loads:
        load.wait()

    def remote(source, target, slot, chunk, device):
        return pltpu.make_async_remote_copy(
            src_ref=source,
            dst_ref=target,
            send_sem=send_sem.at[slot, chunk],
            recv_sem=recv_sem.at[slot, chunk],
            device_id=device,
            device_id_type=pl.DeviceIdType.MESH,
        )

    def span(chunk):
        return pl.ds(STARTS[chunk], SIZES[chunk])

    def far(kind, slot, chunk):
        device = tuple(jnp.where(kind == 0, b, a) for a, b in zip(after, before))
        return remote(own.at[kind, span(chunk)], held[chunk].at[slot], slot, chunk, device)

    first, second = side, 1 - side
    chunks = range(CHUNKS)

    def passed(source, slot, device):
        return [remote(held[i].at[source], held[i].at[slot], slot, i, device) for i in chunks]

    far_stream = [far(first, FAR_FIRST, i) for i in chunks] + [far(second, FAR_SECOND, i) for i in chunks]
    near_stream = [remote(own.at[1 - side, span(i)], held[i].at[NEAR_OWN], NEAR_OWN, i, near) for i in chunks]
    near_stream += passed(FAR_FIRST, NEAR_FAR, near)
    twin_stream = passed(NEAR_OWN, CORE_NEAR_OWN, twin) + passed(NEAR_FAR, CORE_NEAR_FAR, twin)
    core_own = [remote(own.at[1 - core, span(i)], twin_held.at[0, span(i)], CORE_OWN, i, twin) for i in chunks]
    far_slot = jnp.where(side == core, FAR_FIRST, FAR_SECOND)
    core_far = [remote(held[i].at[far_slot], twin_held.at[1, span(i)], CORE_FAR, i, twin) for i in chunks]

    far_first, far_second = far_stream[:CHUNKS], far_stream[CHUNKS:]
    near_own, near_far = near_stream[:CHUNKS], near_stream[CHUNKS:]

    for i in chunks:
        far_first[i].start()
        near_own[i].start()
    for i in chunks:
        core_own[i].start()

    scale = jnp.exp(jnp.full((1, rows), log_scale_ref[0], jnp.float32))
    offset = bias_ref[0]
    for kind in range(2):
        turned[kind] = own[kind].T

    def weights_of(block, kind):
        inner = jnp.dot(block, turned[1 - kind], preferred_element_type=jnp.float32)
        return jax.nn.sigmoid(scale * inner + offset)

    def add(block, kind):
        weights = (scale * weights_of(block, kind)).astype(jnp.bfloat16)
        total[1 - kind] += lax.dot_general(
            weights, block, (((0,), (0,)), ((), ())), preferred_element_type=jnp.float32
        )

    def add_batch(step):
        twin_stream[step].wait_recv()
        chunk, late = step % CHUNKS, step // CHUNKS
        block = held[chunk][3 * late : 3 * late + 3].reshape(3 * SIZES[chunk], width)
        add(block, second if late else first)

    row_ids = lax.broadcasted_iota(jnp.int32, (rows, rows), 0)
    col_ids = lax.broadcasted_iota(jnp.int32, (rows, rows), 1)
    target = jnp.where(row_ids == col_ids, 1.0, 0.0).astype(jnp.float32)
    own_weights = (scale * (weights_of(own[0], 0) - target)).astype(jnp.bfloat16)
    total[0] = jnp.dot(own_weights, own[1], preferred_element_type=jnp.float32)
    total[1] = lax.dot_general(own_weights, own[0], (((0,), (0,)), ((), ())), preferred_element_type=jnp.float32)

    for copy in core_own:
        copy.wait_recv()
    add(twin_held[0], core)
    for copy in far_second:
        copy.start()

    for i in chunks:
        far_first[i].wait_recv()
        near_far[i].start()

        @pl.when(side == core)
        def _():
            core_far[i].start()

    for i in chunks:
        near_own[i].wait_recv()
        twin_stream[i].start()

    for i in chunks:
        add_batch(i)
    for i in chunks:
        near_far[i].wait_recv()
        twin_stream[CHUNKS + i].start()
        far_second[i].wait_recv()

        @pl.when(side != core)
        def _():
            core_far[i].start()

        if i > 0:
            add_batch(CHUNKS + i - 1)

    for copy in core_far:
        copy.wait_recv()
    add(twin_held[1], 1 - core)
    add_batch(2 * CHUNKS - 1)

    for copies in (far_stream, near_stream, twin_stream, core_own, core_far):
        for copy in copies:
            copy.wait_send()


def write_out(total, image_out, text_out, store_sem):
    stores = [
        pltpu.make_async_copy(total.at[0], image_out, store_sem.at[0]),
        pltpu.make_async_copy(total.at[1], text_out, store_sem.at[1]),
    ]
    for store in stores:
        store.start()
    for store in stores:
        store.wait()


def local(image_emb, text_emb, log_scale, bias):
    rows, width = image_emb.shape
    block = jax.ShapeDtypeStruct((rows, width), jnp.float32)
    assert rows == sum(SIZES)
    in_hbm = [pltpu.with_memory_space_constraint(value, pltpu.HBM) for value in (image_emb, text_emb)]
    total = pl.pallas_call(
        kernel,
        out_shape=pltpu.VMEM((2, rows, width), jnp.float32),
        in_specs=[pl.BlockSpec(memory_space=pltpu.SMEM)] * 2 + [pl.BlockSpec(memory_space=pl.ANY)] * 2,
        out_specs=pl.BlockSpec(memory_space=pltpu.VMEM),
        scratch_shapes=[
            pltpu.VMEM((2, rows, width), jnp.bfloat16),
            pltpu.VMEM((2, width, rows), jnp.bfloat16),
            *[pltpu.VMEM((6, size, width), jnp.bfloat16) for size in SIZES],
            pltpu.VMEM((2, rows, width), jnp.bfloat16),
            pltpu.SemaphoreType.DMA((2,)),
            pltpu.SemaphoreType.DMA((8, CHUNKS)),
            pltpu.SemaphoreType.DMA((8, CHUNKS)),
        ],
        compiler_params=pltpu.CompilerParams(
            collective_id=0, has_side_effects=True, vmem_limit_bytes=32 * 1024 * 1024
        ),
        cost_estimate=pl.CostEstimate(
            flops=20 * 2 * rows * rows * width, bytes_accessed=12 * rows * width, transcendentals=9 * rows * rows
        ),
    )(log_scale, bias, *in_hbm)
    return pl.pallas_call(
        write_out,
        out_shape=(block, block),
        in_specs=[pl.BlockSpec(memory_space=pl.ANY)],
        out_specs=(pl.BlockSpec(memory_space=pl.ANY), pl.BlockSpec(memory_space=pl.ANY)),
        scratch_shapes=[pltpu.SemaphoreType.DMA((2,))],
        compiler_params=pltpu.CompilerParams(vmem_limit_bytes=1024 * 1024),
        cost_estimate=pl.CostEstimate(flops=0, bytes_accessed=16 * rows * width, transcendentals=0),
    )(total)


def solution(mesh):
    count = 1
    for axis in ("dp", "mp"):
        count *= mesh.shape[axis]
    assert mesh.shape["mp"] % 4 == 0 and count > 2 * SHIFTS
    return jax.shard_map(
        local,
        mesh=mesh,
        in_specs=(P(("dp", "mp"), None), P(("dp", "mp"), None), P(), P()),
        out_specs=(P(("dp", "mp"), None), P(("dp", "mp"), None)),
        check_vma=False,
    )
```

```python
import jax
import jax.numpy as jnp
from jax import lax
from jax.experimental import pallas as pl
from jax.experimental.pallas import tpu as pltpu
from jax.sharding import PartitionSpec as P

SHIFTS = 4
SIZES = (96, 96)
STARTS = (0, 96)
CHUNKS = len(SIZES)

FAR_FIRST = 0
NEAR_OWN = 1
CORE_NEAR_OWN = 2
FAR_SECOND = 3
NEAR_FAR = 4
CORE_NEAR_FAR = 5
CORE_OWN = 6
CORE_FAR = 7


def kernel(
    log_scale_ref, bias_ref, image_ref, text_ref, total,
    own, turned, *scratch,
):
    dp_count, mp_count = lax.axis_size("dp"), lax.axis_size("mp")
    count = dp_count * mp_count
    me = lax.axis_index("dp") * mp_count + lax.axis_index("mp")
    core = lax.rem(me, 2)
    side = lax.rem(me // 2, 2)
    rows, width = image_ref.shape
    held = scratch[:CHUNKS]
    twin_held, load_sem, send_sem, recv_sem = scratch[CHUNKS:]

    def place(index):
        return (index // mp_count, lax.rem(index, mp_count))

    after = place(lax.rem(me + SHIFTS, count))
    before = place(lax.rem(me + count - SHIFTS, count))
    near = place(me + 2 - 4 * side)
    twin = place(me + 1 - 2 * core)

    loads = [
        pltpu.make_async_copy(image_ref, own.at[0], load_sem.at[0]),
        pltpu.make_async_copy(text_ref, own.at[1], load_sem.at[1]),
    ]
    for load in loads:
        load.start()

    barrier = pltpu.get_barrier_semaphore()
    for other in (after, before, near, twin):
        pl.semaphore_signal(barrier, inc=1, device_id=other, device_id_type=pl.DeviceIdType.MESH)
    pl.semaphore_wait(barrier, 4)
    for load in loads:
        load.wait()

    def remote(source, target, slot, chunk, device):
        return pltpu.make_async_remote_copy(
            src_ref=source,
            dst_ref=target,
            send_sem=send_sem.at[slot, chunk],
            recv_sem=recv_sem.at[slot, chunk],
            device_id=device,
            device_id_type=pl.DeviceIdType.MESH,
        )

    def span(chunk):
        return pl.ds(STARTS[chunk], SIZES[chunk])

    def far(kind, slot, chunk):
        device = tuple(jnp.where(kind == 0, b, a) for a, b in zip(after, before))
        return remote(own.at[kind, span(chunk)], held[chunk].at[slot], slot, chunk, device)

    first, second = side, 1 - side
    chunks = range(CHUNKS)

    def passed(source, slot, device):
        return [remote(held[i].at[source], held[i].at[slot], slot, i, device) for i in chunks]

    far_stream = [far(first, FAR_FIRST, i) for i in chunks] + [far(second, FAR_SECOND, i) for i in chunks]
    near_stream = [remote(own.at[1 - side, span(i)], held[i].at[NEAR_OWN], NEAR_OWN, i, near) for i in chunks]
    near_stream += passed(FAR_FIRST, NEAR_FAR, near)
    twin_stream = passed(NEAR_OWN, CORE_NEAR_OWN, twin) + passed(NEAR_FAR, CORE_NEAR_FAR, twin)
    core_own = [remote(own.at[1 - core, span(i)], twin_held.at[0, span(i)], CORE_OWN, i, twin) for i in chunks]
    far_slot = jnp.where(side == core, FAR_FIRST, FAR_SECOND)
    core_far = [remote(held[i].at[far_slot], twin_held.at[1, span(i)], CORE_FAR, i, twin) for i in chunks]

    far_first, far_second = far_stream[:CHUNKS], far_stream[CHUNKS:]
    near_own, near_far = near_stream[:CHUNKS], near_stream[CHUNKS:]

    for i in chunks:
        far_first[i].start()
        near_own[i].start()
    for i in chunks:
        far_second[i].start()
        core_own[i].start()

    scale = jnp.exp(jnp.full((1, rows), log_scale_ref[0], jnp.float32))
    offset = bias_ref[0]
    for kind in range(2):
        turned[kind] = own[kind].T

    def weights_of(block, kind):
        inner = jnp.dot(block, turned[1 - kind], preferred_element_type=jnp.float32)
        return jax.nn.sigmoid(scale * inner + offset)

    def add(block, kind):
        weights = (scale * weights_of(block, kind)).astype(jnp.bfloat16)
        total[1 - kind] += lax.dot_general(
            weights, block, (((0,), (0,)), ((), ())), preferred_element_type=jnp.float32
        )

    def add_batch(step):
        twin_stream[step].wait_recv()
        chunk, late = step % CHUNKS, step // CHUNKS
        block = held[chunk][3 * late : 3 * late + 3].reshape(3 * SIZES[chunk], width)
        add(block, second if late else first)

    row_ids = lax.broadcasted_iota(jnp.int32, (rows, rows), 0)
    col_ids = lax.broadcasted_iota(jnp.int32, (rows, rows), 1)
    target = jnp.where(row_ids == col_ids, 1.0, 0.0).astype(jnp.float32)
    own_weights = (scale * (weights_of(own[0], 0) - target)).astype(jnp.bfloat16)
    total[0] = jnp.dot(own_weights, own[1], preferred_element_type=jnp.float32)
    total[1] = lax.dot_general(own_weights, own[0], (((0,), (0,)), ((), ())), preferred_element_type=jnp.float32)

    for copy in core_own:
        copy.wait_recv()
    add(twin_held[0], core)

    for i in chunks:
        far_first[i].wait_recv()
        near_far[i].start()

        @pl.when(side == core)
        def _():
            core_far[i].start()

    for i in chunks:
        near_own[i].wait_recv()
        twin_stream[i].start()

    for i in chunks:
        add_batch(i)
    for i in chunks:
        near_far[i].wait_recv()
        twin_stream[CHUNKS + i].start()
        far_second[i].wait_recv()

        @pl.when(side != core)
        def _():
            core_far[i].start()

        if i > 0:
            add_batch(CHUNKS + i - 1)

    for copy in core_far:
        copy.wait_recv()
    add(twin_held[1], 1 - core)
    add_batch(2 * CHUNKS - 1)

    for copies in (far_stream, near_stream, twin_stream, core_own, core_far):
        for copy in copies:
            copy.wait_send()


def write_out(total, image_out, text_out, store_sem):
    stores = [
        pltpu.make_async_copy(total.at[0], image_out, store_sem.at[0]),
        pltpu.make_async_copy(total.at[1], text_out, store_sem.at[1]),
    ]
    for store in stores:
        store.start()
    for store in stores:
        store.wait()


def local(image_emb, text_emb, log_scale, bias):
    rows, width = image_emb.shape
    block = jax.ShapeDtypeStruct((rows, width), jnp.float32)
    assert rows == sum(SIZES)
    in_hbm = [pltpu.with_memory_space_constraint(value, pltpu.HBM) for value in (image_emb, text_emb)]
    total = pl.pallas_call(
        kernel,
        out_shape=pltpu.VMEM((2, rows, width), jnp.float32),
        in_specs=[pl.BlockSpec(memory_space=pltpu.SMEM)] * 2 + [pl.BlockSpec(memory_space=pl.ANY)] * 2,
        out_specs=pl.BlockSpec(memory_space=pltpu.VMEM),
        scratch_shapes=[
            pltpu.VMEM((2, rows, width), jnp.bfloat16),
            pltpu.VMEM((2, width, rows), jnp.bfloat16),
            *[pltpu.VMEM((6, size, width), jnp.bfloat16) for size in SIZES],
            pltpu.VMEM((2, rows, width), jnp.bfloat16),
            pltpu.SemaphoreType.DMA((2,)),
            pltpu.SemaphoreType.DMA((8, CHUNKS)),
            pltpu.SemaphoreType.DMA((8, CHUNKS)),
        ],
        compiler_params=pltpu.CompilerParams(
            collective_id=0, has_side_effects=True, vmem_limit_bytes=32 * 1024 * 1024
        ),
        cost_estimate=pl.CostEstimate(
            flops=20 * 2 * rows * rows * width, bytes_accessed=12 * rows * width, transcendentals=9 * rows * rows
        ),
    )(log_scale, bias, *in_hbm)
    return pl.pallas_call(
        write_out,
        out_shape=(block, block),
        in_specs=[pl.BlockSpec(memory_space=pl.ANY)],
        out_specs=(pl.BlockSpec(memory_space=pl.ANY), pl.BlockSpec(memory_space=pl.ANY)),
        scratch_shapes=[pltpu.SemaphoreType.DMA((2,))],
        compiler_params=pltpu.CompilerParams(vmem_limit_bytes=1024 * 1024),
        cost_estimate=pl.CostEstimate(flops=0, bytes_accessed=16 * rows * width, transcendentals=0),
    )(total)


def solution(mesh):
    count = 1
    for axis in ("dp", "mp"):
        count *= mesh.shape[axis]
    assert mesh.shape["mp"] % 4 == 0 and count > 2 * SHIFTS
    return jax.shard_map(
        local,
        mesh=mesh,
        in_specs=(P(("dp", "mp"), None), P(("dp", "mp"), None), P(), P()),
        out_specs=(P(("dp", "mp"), None), P(("dp", "mp"), None)),
        check_vma=False,
    )
```
